32 devices in a mesh: sens: 1, samp: 32 (over z, y, x, core).
Axes of the slice: x: 2, y: 2, z: 4, core: 2. Of those that a mesh axis runs over, the one named last changes fastest.
Arguments:
- slopes: bfloat16 [2, 128, 37632], P(None, 'samp', 'sens'), may hold values from -0.0625 to 0.0625
- targets: bfloat16 [2, 8192, 128], P(None, 'samp'), may hold values from -6 to 6
- reconstructor: float32 [1, 32, 32, 128, 128], P('sens', 'samp'), may hold values from -6 to 6
- foot_act: int32 [1, 32, 32], P('sens'), may hold values from 0 to 1, as said below
- foot_slope: int32 [1, 32, 32], P('sens'), may hold values from 0 to 293, as said below
- foot_count: int32 [1, 32], P('sens'), may hold values from 16 to 32, as said below
Outputs:
- fitted: float32 [1, 32, 32, 128, 128], P('sens', 'samp')
- fit_residual: bfloat16 [8192, 128], P('samp')
The draws below stay inside these ranges and needn't reach their ends.
Inputs may be any that keep to these rules, and one draw needn't show every extreme that they name: `foot_act`: slots 0 to foot_count-1 of a device are live, the rest padding (actuator block 0 and a slope block already named by slot 0); no (actuator block, slope block) pair repeats among live slots; the slope blocks of one actuator block form a run of consecutive blocks modulo 294. `foot_slope`: the live slots of one device name at most 20 distinct slope blocks; for every sens index some device names exactly 20. `foot_count`: for every sens index some device has 32 live slots.
All inputs are finite; a program needn't handle non-finite values.
Results may differ from the reference program's by a relative error of at most 0.0037.
Values may be sent and summed in bfloat16 or wider, within the bound.
No kernel may reach another device: no remote copies, remote signals or barrier semaphores. Data moves between devices by JAX's collectives and lax.ppermute only.
A program may use at most 64 MiB of HBM per device.

```python
import jax
import jax.numpy as jnp
from jax import lax

SB = 128
ACT_DEV = 2
SGB = 294
K_MAX = 32
DIST_MAX = 20
STEPS = 2
SLOPES = 37632
ACTUATORS = 8192
SAMPLES = 128
N_SENS = 1
N_SAMP = 32


def footprint_tables(key):
    base_key = jax.random.fold_in(key, 7331)
    keys = jax.random.split(base_key, 5)
    grid_shape = (N_SENS, N_SAMP)
    first_len = jax.random.randint(keys[0], grid_shape, K_MAX // 4, K_MAX // 2 + 1)
    second_len = jax.random.randint(keys[1], grid_shape, K_MAX // 4, K_MAX // 2 + 1)
    start_block = jax.random.randint(keys[2], grid_shape, 0, SGB)
    offset = jax.random.randint(keys[3], grid_shape, 0, DIST_MAX - K_MAX // 2 + 1)
    forced = jax.random.randint(keys[4], (N_SENS,), 0, N_SAMP)
    is_forced = jnp.arange(N_SAMP)[None, :] == forced[:, None]
    first_len = jnp.where(is_forced, K_MAX // 2, first_len)
    second_len = jnp.where(is_forced, K_MAX // 2, second_len)
    offset = jnp.where(is_forced, DIST_MAX - K_MAX // 2, offset)
    slot_ids = jnp.arange(K_MAX)[None, None, :]
    first_end = first_len[:, :, None]
    in_first = slot_ids < first_end
    in_second = (slot_ids >= first_end) & (slot_ids < first_end + second_len[:, :, None])
    start_col = start_block[:, :, None]
    act_table = jnp.where(in_second, 1, 0).astype(jnp.int32)
    slope_table = jnp.where(in_first, start_col + slot_ids, jnp.where(in_second, start_col + offset[:, :, None] + slot_ids - first_end, start_col))
    slope_table = (slope_table % SGB).astype(jnp.int32)
    count_table = (first_len + second_len).astype(jnp.int32)
    return (act_table, slope_table, count_table)


def draw_foot_act(key, part):
    return footprint_tables(key)[0]


def draw_foot_slope(key, part):
    return footprint_tables(key)[1]


def draw_foot_count(key, part):
    return footprint_tables(key)[2]


def level_of(key, dims, shards, low, high):
    gain = 1.0
    for axis_at, shards_of in shards:
        steps = jax.random.uniform(jax.random.fold_in(jax.random.fold_in(key, 6), axis_at), (shards_of,), jnp.float32, low / len(shards), high / len(shards))
        gain = gain * jnp.repeat(jnp.exp(steps), dims[axis_at] // shards_of).reshape((-1,) + (1,) * (len(dims) - 1 - axis_at))
    return gain


def bell_draw(key, extent, width, most, cuts=(), dtype=jnp.bfloat16):
    entries = width * jax.random.normal(key, extent, jnp.float32)
    if cuts:
        entries = entries * level_of(key, extent, cuts, -0.22, 0.18)
    return jnp.clip(entries, -most, most).astype(dtype)


def setup_inputs(seed: int = 0) -> dict:
    key_list = jax.random.split(jax.random.key(seed), 7)
    slopes = bell_draw(key_list[0], (STEPS, SAMPLES, SLOPES), (2 * K_MAX * SB) ** -0.5, 0.0625, ((1, 32),))
    targets = bell_draw(key_list[1], (STEPS, ACTUATORS, SAMPLES), 1.0, 6.0, ((1, 32),))
    reconstructor = bell_draw(key_list[2], (N_SENS, N_SAMP, K_MAX, SB, SB), 1.0, 6.0, ((1, 32),), jnp.float32)
    foot_act = draw_foot_act(jax.random.fold_in(key_list[6], 71), 0)
    foot_slope = draw_foot_slope(jax.random.fold_in(key_list[6], 71), 0)
    foot_count = draw_foot_count(jax.random.fold_in(key_list[6], 71), 0)
    return {"slopes": slopes, "targets": targets, "reconstructor": reconstructor, "foot_act": foot_act, "foot_slope": foot_slope, "foot_count": foot_count}


def reference(slopes, targets, reconstructor, foot_act, foot_slope, foot_count):
    step_rate = K_MAX * SB / (SAMPLES + 3 * K_MAX * SB)
    live_slots = jnp.arange(K_MAX)[None, None, :] < foot_count[:, :, None]
    act_onehot = ((foot_act[:, :, None, :] == jnp.arange(ACT_DEV)[None, None, :, None])
                  & live_slots[:, :, None, :]).astype(jnp.float32)
    sens_ids = jnp.arange(N_SENS)
    weights = jnp.transpose(reconstructor, (1, 0, 2, 3, 4))
    slope_by_dev = jnp.transpose(foot_slope, (1, 0, 2))
    act_by_dev = jnp.transpose(foot_act, (1, 0, 2))
    live_by_dev = jnp.transpose(live_slots, (1, 0, 2))
    onehot_by_dev = jnp.transpose(act_onehot, (1, 0, 2, 3))
    residuals = None
    for step in range(STEPS):
        slope_blocks = slopes[step].reshape(SAMPLES, N_SENS, SGB, SB)
        target_blocks = targets[step].reshape(N_SAMP, ACT_DEV, SB, SAMPLES)

        def device_update(device_items):
            weights_dev, slope_dev, onehot_dev, live_dev, act_dev, target_dev = device_items
            picked = slope_blocks[:, sens_ids[:, None], slope_dev, :].astype(jnp.float32)
            weights_low = weights_dev.astype(jnp.bfloat16).astype(jnp.float32)
            partial_sums = jnp.einsum('skil,nskl->skin', weights_low, picked)
            prediction = jnp.einsum('sjk,skin->jin', onehot_dev, partial_sums,
                                    precision=lax.Precision.HIGHEST)
            residual = (prediction - target_dev.astype(jnp.float32)).astype(jnp.bfloat16)
            slot_residual = residual[act_dev].astype(jnp.float32)
            gradient = jnp.einsum('skin,nskl->skil', slot_residual, picked)
            updated = jnp.where(live_dev[:, :, None, None], weights_dev - step_rate * gradient, weights_dev)
            return updated, residual

        weights, residuals = lax.map(device_update, (weights, slope_by_dev, onehot_by_dev,
                                                     live_by_dev, act_by_dev, target_blocks))
    fitted = jnp.transpose(weights, (1, 0, 2, 3, 4))
    return fitted, residuals.reshape(ACTUATORS, SAMPLES)
```

```python
import functools

import jax
import jax.numpy as jnp
from jax import lax
from jax.experimental import pallas as pl
from jax.experimental.pallas import tpu as pltpu
from jax.sharding import PartitionSpec as P

STEPS = 2
DISTINCT = 20
MIB = 1 << 20


def window_starts(slope_all, count_all, groups):
    slots = slope_all.shape[1]
    half = groups // 2
    live = jnp.arange(slots)[None, :] < count_all[:, None]
    turned = jnp.where(slope_all >= groups - half, slope_all - (groups - half), slope_all + half)

    def span(blocks):
        low = jnp.min(jnp.where(live, blocks, groups), axis=1)
        high = jnp.max(jnp.where(live, blocks, -1), axis=1)
        return low, high - low < DISTINCT

    low, fits = span(slope_all)
    low_turned, fits_turned = span(turned)
    unturned = jnp.where(low_turned >= half, low_turned - half, low_turned + groups - half)
    return jnp.where(fits, low, jnp.where(fits_turned, unturned, -1)).astype(jnp.int32)


def own_places(slopes_own, count_own, start, groups):
    slots = slopes_own.shape[0]
    ids = jnp.arange(slots)
    live = ids < count_own
    same = (slopes_own[:, None] == slopes_own[None, :]) & live[None, :]
    repeated = jnp.any(same & (ids[None, :] < ids[:, None]), axis=1)
    first = live & ~repeated
    rank = jnp.sum(first[None, :] & (ids[None, :] < ids[:, None]), axis=1)
    ranked = jnp.sum(jnp.where(same & first[None, :], rank[None, :], 0), axis=1)
    offset = slopes_own - start
    offset = jnp.where(offset < 0, offset + groups, offset)
    return jnp.where(live, jnp.where(start >= 0, offset, ranked), -1).astype(jnp.int32)


def pack_kernel(starts, slope_tab, counts, slopes, out, rows, sems):
    steps, samp_dev, width = slopes.shape
    block = 128
    groups = width // block
    devices, _, window = out.shape
    span = window // block

    def join(first, last):
        cols = slice(first * block, last * block)
        return jnp.concatenate([slopes[t, :, cols] for t in range(steps)], axis=0)

    piece = 14
    for first in range(0, groups, piece):
        last = min(first + piece, groups)
        rows[:, first * block : last * block] = join(first, last)
    rows[:, width:] = join(0, span)

    def window_of(d):
        return pltpu.make_async_copy(
            rows.at[:, pl.ds(pl.multiple_of(starts[d] * block, block), window)], out.at[d], sems.at[d]
        )

    def block_to(d, group, at):
        return pltpu.make_async_copy(
            rows.at[:, pl.ds(pl.multiple_of(group * block, block), block)],
            out.at[d, :, pl.ds(pl.multiple_of(at * block, block), block)],
            sems.at[d],
        )

    def one_by_one(d):
        def slot(k, placed):
            group = slope_tab[d, k]
            seen = lax.fori_loop(
                0, k, lambda j, s: jnp.where(slope_tab[d, j] == group, 1, s), jnp.int32(0)
            )

            @pl.when(seen == 0)
            def _():
                block_to(d, group, placed).start()

            return placed + 1 - seen

        placed = lax.fori_loop(0, counts[d], slot, jnp.int32(0))

        def fill(j, carry):
            block_to(d, slope_tab[d, 0], j).start()
            return carry

        lax.fori_loop(placed, span, fill, 0)

    def send(d, carry):
        @pl.when(starts[d] >= 0)
        def _():
            window_of(d).start()

        @pl.when(starts[d] < 0)
        def _():
            one_by_one(d)

        return carry

    lax.fori_loop(0, devices, send, 0)

    def settle(d, carry):
        pltpu.make_async_copy(rows.at[:, pl.ds(0, window)], out.at[d], sems.at[d]).wait()
        return carry

    lax.fori_loop(0, devices, settle, 0)


def pack(starts, slope_all, count_all, slopes):
    steps, samp_dev, width = slopes.shape
    devices = slope_all.shape[0]
    block = 128
    tall = steps * samp_dev
    window = DISTINCT * block
    smem = pl.BlockSpec(memory_space=pltpu.SMEM)
    return pl.pallas_call(
        pack_kernel,
        out_shape=jax.ShapeDtypeStruct((devices, tall, window), slopes.dtype),
        in_specs=[smem, smem, smem, pl.BlockSpec(memory_space=pltpu.VMEM)],
        out_specs=pl.BlockSpec(memory_space=pl.ANY),
        scratch_shapes=[
            pltpu.VMEM((tall, width + window), slopes.dtype),
            pltpu.SemaphoreType.DMA((devices,)),
        ],
        compiler_params=pltpu.CompilerParams(vmem_limit_bytes=16 * MIB),
        name="pack_windows",
    )(starts, slope_all, count_all, slopes)


def stage_kernel(rate, samp_dev, places, acts, weights, targets, stack, low, spread, rates):
    steps, rows, samples = targets.shape
    slots, block, _ = weights.shape
    stack[...] = jnp.zeros_like(stack)
    low[...] = jnp.zeros_like(low)
    rates[...] = jnp.zeros_like(rates)

    def slot(k, carry):
        @pl.when(places[k] >= 0)
        def _():
            at_rows = pl.ds(pl.multiple_of(acts[k] * block, block), block)
            at_cols = pl.ds(pl.multiple_of(places[k] * block, block), block)
            now = weights[k]
            stack[at_rows, at_cols] = now
            low[at_rows, at_cols] = now.astype(low.dtype)
            rates[acts[k], :, at_cols] = jnp.full((8, block), rate, rates.dtype)

        return carry

    lax.fori_loop(0, slots, slot, 0)
    wide = spread.shape[2]
    for t in range(steps):
        spread[t] = jnp.dot(
            targets[t], spreader(samples, wide, samp_dev, t, targets.dtype), preferred_element_type=jnp.float32
        )


def spreader(samples, wide, samp_dev, step, dtype):
    tall = wide * samp_dev // samples
    n = lax.broadcasted_iota(jnp.int32, (samples, wide), 0)
    c = lax.broadcasted_iota(jnp.int32, (samples, wide), 1)
    column = (n // samp_dev) * tall + step * samp_dev + n % samp_dev
    return (c == column).astype(jnp.float32).astype(dtype)


def stage(rate, samp_dev, places, acts, weights, targets):
    steps, rows, samples = targets.shape
    block = weights.shape[-1]
    window = DISTINCT * block
    smem = pl.BlockSpec(memory_space=pltpu.SMEM)
    vmem = pl.BlockSpec(memory_space=pltpu.VMEM)
    return pl.pallas_call(
        functools.partial(stage_kernel, rate, samp_dev),
        out_shape=[
            jax.ShapeDtypeStruct((rows, window), jnp.float32),
            jax.ShapeDtypeStruct((rows, window), jnp.bfloat16),
            jax.ShapeDtypeStruct((steps, rows, steps * samples), jnp.float32),
            jax.ShapeDtypeStruct((rows // block, 8, window), jnp.float32),
        ],
        in_specs=[smem, smem, vmem, vmem],
        out_specs=[vmem, vmem, vmem, vmem],
        compiler_params=pltpu.CompilerParams(vmem_limit_bytes=16 * MIB),
        cost_estimate=pl.CostEstimate(flops=10**8, bytes_accessed=9 * 10**6, transcendentals=0),
        name="stage_weights",
    )(places, acts, weights, targets)


def fit_kernel(
    samp_dev, places, acts, seen, stack_in, low_in, spread, rates, weights, fitted, residual, stack, low, slot_of, sems
):
    steps, rows, wide = spread.shape
    slots, block, _ = weights.shape
    window = seen.shape[1]
    span = window // block
    blocks = rows // block
    samples = residual.shape[1]
    tall = wide * samp_dev // samples

    def clear(j, carry):
        slot_of[j] = -1
        return carry

    lax.fori_loop(0, blocks * span, clear, 0)

    def note(k, carry):
        @pl.when(places[k] >= 0)
        def _():
            slot_of[acts[k] * span + places[k]] = k

        @pl.when(places[k] < 0)
        def _():
            pltpu.make_async_copy(weights.at[k], fitted.at[k], sems.at[k]).start()

        return carry

    lax.fori_loop(0, slots, note, 0)

    column = lax.broadcasted_iota(jnp.int32, (rows, wide), 1)
    step_of = (column % tall) // samp_dev
    chunk = 4 * block
    for t in range(steps):
        source = low_in if t == 0 else low
        held = stack_in if t == 0 else stack
        predicted = lax.dot_general(
            source[...], seen[...], (((1,), (1,)), ((), ())), preferred_element_type=jnp.float32
        )
        rest = jnp.where(step_of == t, predicted - spread[t], 0.0).astype(jnp.bfloat16)
        if t == steps - 1:
            pick = spreader(samples, wide, samp_dev, t, jnp.bfloat16)
            residual[...] = lax.dot_general(
                rest, pick, (((1,), (1,)), ((), ())), preferred_element_type=jnp.float32
            ).astype(residual.dtype)
        for first in range(0, window, chunk):
            cols = slice(first, min(first + chunk, window))
            gradient = jnp.dot(rest, seen[:, cols], preferred_element_type=jnp.float32)
            for a in range(blocks):
                at = slice(a * block, (a + 1) * block)
                new = held[at, cols] - rates[a, 0:1, cols] * gradient[at]
                stack[at, cols] = new
                if t < steps - 1:
                    low[at, cols] = new.astype(low.dtype)
            if t == steps - 1:
                for a in range(blocks):
                    for p in range(first // block, cols.stop // block):
                        k = slot_of[a * span + p]

                        @pl.when(k >= 0)
                        def _(a=a, p=p, k=k):
                            pltpu.make_async_copy(
                                stack.at[pl.ds(a * block, block), pl.ds(p * block, block)], fitted.at[k], sems.at[k]
                            ).start()

    def settle(k, carry):
        pltpu.make_async_copy(stack.at[pl.ds(0, block), pl.ds(0, block)], fitted.at[k], sems.at[k]).wait()
        return carry

    lax.fori_loop(0, slots, settle, 0)


def fit(samp_dev, places, acts, seen, stack, low, spread, rates, weights, samples):
    rows, window = stack.shape
    slots, block, _ = weights.shape
    smem = pl.BlockSpec(memory_space=pltpu.SMEM)
    vmem = pl.BlockSpec(memory_space=pltpu.VMEM)
    anywhere = pl.BlockSpec(memory_space=pl.ANY)
    return pl.pallas_call(
        functools.partial(fit_kernel, samp_dev),
        out_shape=[
            jax.ShapeDtypeStruct(weights.shape, jnp.float32),
            jax.ShapeDtypeStruct((rows, samples), jnp.bfloat16),
        ],
        in_specs=[smem, smem, vmem, vmem, vmem, vmem, vmem, anywhere],
        out_specs=[anywhere, vmem],
        scratch_shapes=[
            pltpu.VMEM((rows, window), jnp.float32),
            pltpu.VMEM((rows, window), jnp.bfloat16),
            pltpu.SMEM((rows // block * DISTINCT,), jnp.int32),
            pltpu.SemaphoreType.DMA((slots,)),
        ],
        compiler_params=pltpu.CompilerParams(vmem_limit_bytes=32 * MIB),
        name="fit_steps",
    )(places, acts, seen, stack, low, spread, rates, weights)


def fit_over_groups(step_rate, samp_dev, places, acts, arrived, weights, targets):
    steps, rows, samples = targets.shape
    slots, block, _ = weights.shape
    live = places >= 0
    devices = arrived.shape[0]
    grouped = arrived.reshape(devices, steps, samp_dev, DISTINCT, block)
    slot_slopes = jnp.take(grouped, jnp.maximum(places, 0), axis=3)
    blocks = rows // block
    onehot = ((acts[None, :] == jnp.arange(blocks)[:, None]) & live[None, :]).astype(jnp.float32)
    residual = None
    for t in range(steps):
        now = slot_slopes[:, t].reshape(samples, slots, block)
        partial_sums = jnp.einsum(
            "kil,nkl->kin", weights.astype(jnp.bfloat16), now, preferred_element_type=jnp.float32
        )
        summed = jnp.einsum("jk,kin->jin", onehot, partial_sums, precision=lax.Precision.HIGHEST)
        total = lax.psum(summed, "sens")
        residual = (total - targets[t].reshape(blocks, block, samples)).astype(jnp.bfloat16)
        gradient = jnp.einsum(
            "kin,nkl->kil", jnp.take(residual, acts, axis=0), now, preferred_element_type=jnp.float32
        )
        weights = jnp.where(live[:, None, None], weights - step_rate * gradient, weights)
    return weights, residual.reshape(rows, samples)


def per_device(slopes, targets, reconstructor, foot_act, foot_slope, foot_count):
    own_index = lax.axis_index("samp")
    block = reconstructor.shape[-1]
    slots = reconstructor.shape[2]
    groups = slopes.shape[2] // block
    samp_dev = slopes.shape[1]
    samples = targets.shape[2]
    devices = foot_slope.shape[1]
    step_rate = slots * block / (samples + 3 * slots * block)
    starts = window_starts(foot_slope[0], foot_count[0], groups)
    packed = pack(starts, foot_slope[0], foot_count[0], slopes)
    arrived = lax.all_to_all(packed, "samp", split_axis=0, concat_axis=0, tiled=True)

    def own(table):
        return lax.dynamic_index_in_dim(table, own_index, 0, keepdims=False)

    places = own_places(own(foot_slope[0]), own(foot_count[0]), own(starts), groups)
    acts = own(foot_act[0])
    weights = reconstructor[0, 0]
    if lax.axis_size("sens") > 1:
        fitted, residual = fit_over_groups(step_rate, samp_dev, places, acts, arrived, weights, targets)
        return fitted[None, None], residual
    stack, low, spread, rates = stage(step_rate, samp_dev, places, acts, weights, targets)
    seen = arrived.reshape(devices * STEPS * samp_dev, DISTINCT * block)
    fitted, residual = fit(samp_dev, places, acts, seen, stack, low, spread, rates, weights, samples)
    return fitted[None, None], residual


def solution(mesh):
    return jax.shard_map(
        per_device,
        mesh=mesh,
        in_specs=(
            P(None, "samp", "sens"),
            P(None, "samp", None),
            P("sens", "samp", None, None, None),
            P("sens", None, None),
            P("sens", None, None),
            P("sens", None),
        ),
        out_specs=(P("sens", "samp", None, None, None), P("samp", None)),
        check_vma=False,
    )
```

```python
import functools

import jax
import jax.numpy as jnp
from jax import lax
from jax.experimental import pallas as pl
from jax.experimental.pallas import tpu as pltpu
from jax.sharding import PartitionSpec as P

STEPS = 2
DISTINCT = 20
BLOCK = 128
MIB = 1 << 20


def own_places(blocks_own, count_own, groups):
    ids = jnp.arange(blocks_own.shape[0])
    half = groups // 2
    turned = jnp.where(blocks_own >= groups - half, blocks_own - (groups - half), blocks_own + half)
    straight = blocks_own - jnp.min(blocks_own)
    around = turned - jnp.min(turned)
    same = blocks_own[:, None] == blocks_own[None, :]
    before = ids[None, :] < ids[:, None]
    first = ~jnp.any(same & before, axis=1)
    rank = jnp.sum(first[None, :] & before, axis=1)
    ranked = jnp.sum(jnp.where(same & first[None, :], rank[None, :], 0), axis=1)
    place = jnp.where(
        jnp.max(straight) < DISTINCT, straight, jnp.where(jnp.max(around) < DISTINCT, around, ranked)
    )
    return jnp.where(ids < count_own, place, -1).astype(jnp.int32)


def pack_kernel(
    pieces, blocks_hbm, slopes, out, blocks_of, raw, rows, row_starts, starts, table, sems, load_sems, small_sems
):
    steps, samp_dev, width = slopes.shape
    groups = width // BLOCK
    devices, _, window = out.shape
    edges = [groups * i // pieces for i in range(pieces + 1)]

    def load(i):
        cols = pl.ds(edges[i] * BLOCK, (edges[i + 1] - edges[i]) * BLOCK)
        return pltpu.make_async_copy(slopes.at[:, :, cols], raw.at[:, :, cols], load_sems.at[i])

    to_vectors = pltpu.make_async_copy(blocks_hbm, blocks_of, small_sems.at[0])
    to_vectors.start()
    for i in range(pieces):
        load(i).start()
    to_vectors.wait()
    blocks = blocks_of[...].astype(jnp.float32)
    half = groups // 2
    turned = jnp.where(blocks >= groups - half, blocks - (groups - half), blocks + half)

    def span(named):
        low = jnp.min(named, axis=1, keepdims=True)
        return low, jnp.max(named, axis=1, keepdims=True) - low < DISTINCT

    low, fits = span(blocks)
    low_turned, fits_turned = span(turned)
    unturned = jnp.where(low_turned >= half, low_turned - half, low_turned + (groups - half))
    first = jnp.where(fits, low, jnp.where(fits_turned, unturned, -1.0))
    lane = lax.broadcasted_iota(jnp.int32, (devices, BLOCK), 1)
    device = lax.broadcasted_iota(jnp.int32, (devices, BLOCK), 0)
    row = jnp.sum(jnp.where(lane == device, jnp.broadcast_to(first, (devices, BLOCK)), 0.0), axis=0, keepdims=True)
    least = jnp.min(row, axis=1, keepdims=True)
    last_lane = lax.broadcasted_iota(jnp.int32, (1, BLOCK), 1) == BLOCK - 1
    row_starts[...] = jnp.where(last_lane, least, row).astype(jnp.int32)
    to_scalars = pltpu.make_async_copy(row_starts, starts, small_sems.at[1])
    to_scalars.start()

    def join(first, last):
        cols = slice(first * BLOCK, last * BLOCK)
        return jnp.concatenate([raw[t, :, cols] for t in range(steps)], axis=0)

    span_blocks = window // BLOCK
    for i in range(pieces):
        load(i).wait()
        for at in range(edges[i], edges[i + 1], 7):
            end = min(at + 7, edges[i + 1])
            rows[:, at * BLOCK : end * BLOCK] = join(at, end)
        if i == 0:
            rows[:, width:] = rows[:, :window]
    to_scalars.wait()

    def to_device(d, group, at, count):
        return pltpu.make_async_copy(
            rows.at[:, pl.ds(pl.multiple_of(group * BLOCK, BLOCK), count * BLOCK)],
            out.at[d, :, pl.ds(pl.multiple_of(at * BLOCK, BLOCK), count * BLOCK)],
            sems.at[d],
        )

    @pl.when(starts[0, BLOCK - 1] >= 0)
    def _():
        for d in range(devices):
            to_device(d, starts[0, d], 0, span_blocks).start()

    @pl.when(starts[0, BLOCK - 1] < 0)
    def _():
        copy_table = pltpu.make_async_copy(blocks_of, table, small_sems.at[2])
        copy_table.start()
        copy_table.wait()

        def one_by_one(d):
            def slot(k, placed):
                group = table[d, k]
                seen = lax.fori_loop(0, k, lambda j, s: jnp.where(table[d, j] == group, 1, s), jnp.int32(0))

                @pl.when(seen == 0)
                def _():
                    to_device(d, group, placed, 1).start()

                return placed + 1 - seen

            placed = lax.fori_loop(0, blocks_of.shape[1], slot, jnp.int32(0))

            def fill(j, carry):
                to_device(d, table[d, 0], j, 1).start()
                return carry

            lax.fori_loop(placed, span_blocks, fill, 0)

        def send(d, carry):
            @pl.when(starts[0, d] >= 0)
            def _():
                to_device(d, starts[0, d], 0, span_blocks).start()

            @pl.when(starts[0, d] < 0)
            def _():
                one_by_one(d)

            return carry

        lax.fori_loop(0, devices, send, 0)

    for d in range(devices):
        to_device(d, 0, 0, span_blocks).wait()


def pack(blocks_of, slopes, pieces=3):
    steps, samp_dev, width = slopes.shape
    devices, slots = blocks_of.shape
    tall = steps * samp_dev
    window = DISTINCT * BLOCK
    return pl.pallas_call(
        functools.partial(pack_kernel, pieces),
        out_shape=pltpu.HBM((devices, tall, window), slopes.dtype),
        in_specs=[pl.BlockSpec(memory_space=pltpu.HBM)] * 2,
        out_specs=pl.BlockSpec(memory_space=pltpu.HBM),
        scratch_shapes=[
            pltpu.VMEM((devices, slots), jnp.int32),
            pltpu.VMEM(slopes.shape, slopes.dtype),
            pltpu.VMEM((tall, width + window), slopes.dtype),
            pltpu.VMEM((1, BLOCK), jnp.int32),
            pltpu.SMEM((1, BLOCK), jnp.int32),
            pltpu.SMEM((devices, slots), jnp.int32),
            pltpu.SemaphoreType.DMA((devices,)),
            pltpu.SemaphoreType.DMA((pieces,)),
            pltpu.SemaphoreType.DMA((3,)),
        ],
        compiler_params=pltpu.CompilerParams(vmem_limit_bytes=16 * MIB),
        name="pack_windows",
    )(pltpu.with_memory_space_constraint(blocks_of, pltpu.HBM), pltpu.with_memory_space_constraint(slopes, pltpu.HBM))


def spreader(samples, wide, samp_dev, step, dtype):
    tall = wide * samp_dev // samples
    n = lax.broadcasted_iota(jnp.int32, (samples, wide), 0)
    c = lax.broadcasted_iota(jnp.int32, (samples, wide), 1)
    column = (n // samp_dev) * tall + step * samp_dev + n % samp_dev
    return (c == column).astype(jnp.float32).astype(dtype)


def fit_kernel(step_rate, samp_dev, holder, seen, weights, targets_hbm, fitted, residual, targets, stack, low, in_sem, out_sems):
    steps, rows, samples = targets.shape
    slots, block, _ = weights.shape
    wide, window = seen.shape
    span = window // block
    blocks = rows // block
    cells = blocks * span
    tall = wide * samp_dev // samples

    load = pltpu.make_async_copy(targets_hbm, targets, in_sem)
    load.start()

    def keep(k, carry):
        pltpu.make_async_copy(weights.at[k], fitted.at[k], out_sems.at[k]).start()
        return carry

    lax.fori_loop(holder[cells], slots, keep, 0)

    def at_rows(a):
        return slice(a * block, (a + 1) * block)

    def at_cols(p):
        return slice(p * block, (p + 1) * block)

    def held(a, p):
        slot = holder[a * span + p]
        return jnp.where(slot >= 0, weights[jnp.maximum(slot, 0)], 0.0)

    for p in range(span):
        for a in range(blocks):
            low[at_rows(a), at_cols(p)] = held(a, p).astype(low.dtype)

    column = lax.broadcasted_iota(jnp.int32, (rows, wide), 1)
    step_of = (column % tall) // samp_dev
    chunk = 4
    for t in range(steps):
        predicted = lax.dot_general(
            low[...], seen[...], (((1,), (1,)), ((), ())), preferred_element_type=jnp.float32
        )
        if t == 0:
            load.wait()
        pick = spreader(samples, wide, samp_dev, t, jnp.bfloat16)
        wanted = jnp.dot(targets[t], pick, preferred_element_type=jnp.float32)
        rest = jnp.where(step_of == t, predicted - wanted, 0.0).astype(jnp.bfloat16)
        if t == steps - 1:
            residual[...] = lax.dot_general(
                rest, pick, (((1,), (1,)), ((), ())), preferred_element_type=jnp.float32
            ).astype(residual.dtype)
        for first in range(0, span, chunk):
            last = min(first + chunk, span)
            gradient = jnp.dot(rest, seen[:, first * block : last * block], preferred_element_type=jnp.float32)
            cell_list = [(a, p) for p in range(first, last) for a in range(blocks)]
            for a, p in cell_list:
                j = a * span + p
                rate = jnp.where(holder[j] >= 0, jnp.float32(step_rate), jnp.float32(0))
                old = held(a, p) if t == 0 else stack[j]
                new = old - rate * gradient[at_rows(a), at_cols(p - first)]
                stack[j] = new
                if t < steps - 1:
                    low[at_rows(a), at_cols(p)] = new.astype(low.dtype)
            if t == steps - 1:
                for a, p in cell_list:
                    j = a * span + p
                    slot = holder[j]

                    @pl.when(slot >= 0)
                    def _(j=j, slot=slot):
                        pltpu.make_async_copy(stack.at[j], fitted.at[slot], out_sems.at[slot]).start()

    def settle(k, carry):
        pltpu.make_async_copy(stack.at[0], fitted.at[k], out_sems.at[k]).wait()
        return carry

    lax.fori_loop(0, slots, settle, 0)


def fit(step_rate, samp_dev, holder, seen, weights, targets):
    steps, rows, samples = targets.shape
    slots, block, _ = weights.shape
    window = seen.shape[1]
    cells = rows // block * DISTINCT
    smem = pl.BlockSpec(memory_space=pltpu.SMEM)
    vmem = pl.BlockSpec(memory_space=pltpu.VMEM)
    hbm = pl.BlockSpec(memory_space=pltpu.HBM)
    return pl.pallas_call(
        functools.partial(fit_kernel, step_rate, samp_dev),
        out_shape=[
            pltpu.HBM(weights.shape, jnp.float32),
            jax.ShapeDtypeStruct((rows, samples), jnp.bfloat16),
        ],
        in_specs=[smem, vmem, vmem, hbm],
        out_specs=[hbm, vmem],
        scratch_shapes=[
            pltpu.VMEM(targets.shape, targets.dtype),
            pltpu.VMEM((cells, block, block), jnp.float32),
            pltpu.VMEM((rows, window), jnp.bfloat16),
            pltpu.SemaphoreType.DMA,
            pltpu.SemaphoreType.DMA((slots,)),
        ],
        compiler_params=pltpu.CompilerParams(vmem_limit_bytes=24 * MIB),
        name="fit_steps",
    )(holder, seen, weights, pltpu.with_memory_space_constraint(targets, pltpu.HBM))


def fit_over_groups(step_rate, samp_dev, places, acts, arrived, weights, targets):
    steps, rows, samples = targets.shape
    slots, block, _ = weights.shape
    live = places >= 0
    devices = arrived.shape[0]
    grouped = arrived.reshape(devices, steps, samp_dev, DISTINCT, block)
    slot_slopes = jnp.take(grouped, jnp.maximum(places, 0), axis=3)
    blocks = rows // block
    onehot = ((acts[None, :] == jnp.arange(blocks)[:, None]) & live[None, :]).astype(jnp.float32)
    residual = None
    for t in range(steps):
        now = slot_slopes[:, t].reshape(samples, slots, block)
        partial_sums = jnp.einsum(
            "kil,nkl->kin", weights.astype(jnp.bfloat16), now, preferred_element_type=jnp.float32
        )
        summed = jnp.einsum("jk,kin->jin", onehot, partial_sums, precision=lax.Precision.HIGHEST)
        total = lax.psum(summed, "sens")
        residual = (total - targets[t].reshape(blocks, block, samples)).astype(jnp.bfloat16)
        gradient = jnp.einsum(
            "kin,nkl->kil", jnp.take(residual, acts, axis=0), now, preferred_element_type=jnp.float32
        )
        weights = jnp.where(live[:, None, None], weights - step_rate * gradient, weights)
    return weights, residual.reshape(rows, samples)


def per_device(slopes, targets, reconstructor, foot_act, foot_slope, foot_count):
    own_index = lax.axis_index("samp")
    block = reconstructor.shape[-1]
    slots = reconstructor.shape[2]
    groups = slopes.shape[2] // block
    samp_dev = slopes.shape[1]
    samples = targets.shape[2]
    devices = foot_slope.shape[1]
    cells = targets.shape[1] // block * DISTINCT
    step_rate = slots * block / (samples + 3 * slots * block)
    packed = pack(foot_slope[0], slopes)
    arrived = lax.all_to_all(packed, "samp", split_axis=0, concat_axis=0, tiled=True)

    def own(table):
        return lax.dynamic_index_in_dim(table, own_index, 0, keepdims=False)

    count = own(foot_count[0])
    places = own_places(own(foot_slope[0]), count, groups)
    acts = own(foot_act[0])
    weights = reconstructor[0, 0]
    if lax.axis_size("sens") > 1:
        fitted, residual = fit_over_groups(step_rate, samp_dev, places, acts, arrived, weights, targets)
        return fitted[None, None], residual
    cell = jnp.where(places >= 0, acts * DISTINCT + places, -1)
    held = cell[None, :] == jnp.arange(cells)[:, None]
    holder = jnp.sum(jnp.where(held, jnp.arange(slots)[None, :] + 1, 0), axis=1) - 1
    holder = jnp.concatenate([holder, count[None]]).astype(jnp.int32)
    seen = arrived.reshape(devices * STEPS * samp_dev, DISTINCT * block)
    fitted, residual = fit(step_rate, samp_dev, holder, seen, weights, targets)
    return fitted[None, None], residual


def solution(mesh):
    return jax.shard_map(
        per_device,
        mesh=mesh,
        in_specs=(
            P(None, "samp", "sens"),
            P(None, "samp", None),
            P("sens", "samp", None, None, None),
            P("sens", None, None),
            P("sens", None, None),
            P("sens", None),
        ),
        out_specs=(P("sens", "samp", None, None, None), P("samp", None)),
        check_vma=False,
    )
```

```python
import functools

import jax
import jax.numpy as jnp
from jax import lax
from jax.experimental import pallas as pl
from jax.experimental.pallas import tpu as pltpu
from jax.sharding import PartitionSpec as P

STEPS = 2
DISTINCT = 20
BLOCK = 128
MIB = 1 << 20


def own_places(blocks_own, count_own, groups):
    ids = jnp.arange(blocks_own.shape[0])
    half = groups // 2
    turned = jnp.where(blocks_own >= groups - half, blocks_own - (groups - half), blocks_own + half)
    straight = blocks_own - jnp.min(blocks_own)
    around = turned - jnp.min(turned)
    same = blocks_own[:, None] == blocks_own[None, :]
    before = ids[None, :] < ids[:, None]
    first = ~jnp.any(same & before, axis=1)
    rank = jnp.sum(first[None, :] & before, axis=1)
    ranked = jnp.sum(jnp.where(same & first[None, :], rank[None, :], 0), axis=1)
    place = jnp.where(
        jnp.max(straight) < DISTINCT, straight, jnp.where(jnp.max(around) < DISTINCT, around, ranked)
    )
    return jnp.where(ids < count_own, place, -1).astype(jnp.int32)


def pack_kernel(pieces, blocks_hbm, slopes, out, blocks_of, rows, starts, table, sems, load_sems, table_sems):
    steps, samp_dev, width = slopes.shape
    groups = width // BLOCK
    devices, _, window = out.shape
    span = window // BLOCK
    slots = blocks_of.shape[1]
    half = groups // 2

    read_table = pltpu.make_async_copy(blocks_hbm, blocks_of, table_sems.at[0])
    read_table.start()
    parts = [(groups * i // pieces, groups * (i + 1) // pieces, 0) for i in range(pieces)] + [(0, span, groups)]
    loads = []
    for i, (first, last, shift) in enumerate(parts):
        for t in range(steps):
            source = slopes.at[t, :, pl.ds(first * BLOCK, (last - first) * BLOCK)]
            target = rows.at[pl.ds(t * samp_dev, samp_dev), pl.ds((first + shift) * BLOCK, (last - first) * BLOCK)]
            loads.append(pltpu.make_async_copy(source, target, load_sems.at[i, t]))
    for load in loads:
        load.start()

    read_table.wait()
    blocks = blocks_of[...].astype(jnp.float32)
    turned = jnp.where(blocks >= groups - half, blocks - (groups - half), blocks + half)

    def extent(named):
        low = jnp.min(named, axis=1, keepdims=True)
        return low, jnp.max(named, axis=1, keepdims=True) - low < DISTINCT

    low, fits = extent(blocks)
    low_turned, fits_turned = extent(turned)
    unturned = jnp.where(low_turned >= half, low_turned - half, low_turned + (groups - half))
    first = jnp.where(fits, low, jnp.where(fits_turned, unturned, -1.0)).astype(jnp.int32)
    first_of = [first[d, 0] for d in range(devices)]
    least = functools.reduce(jnp.minimum, first_of)
    for load in loads:
        load.wait()

    def to_device(d, group, at, count):
        return pltpu.make_async_copy(
            rows.at[:, pl.ds(pl.multiple_of(group * BLOCK, BLOCK), count * BLOCK)],
            out.at[d, :, pl.ds(pl.multiple_of(at * BLOCK, BLOCK), count * BLOCK)],
            sems.at[d],
        )

    @pl.when(least >= 0)
    def _():
        for d in range(devices):
            to_device(d, first_of[d], 0, span).start()

    @pl.when(least < 0)
    def _():
        for d in range(devices):
            starts[d] = first_of[d]
        copy_table = pltpu.make_async_copy(blocks_of, table, table_sems.at[1])
        copy_table.start()
        copy_table.wait()

        def one_by_one(d):
            def slot(k, placed):
                group = table[d, k]
                seen = lax.fori_loop(0, k, lambda j, s: jnp.where(table[d, j] == group, 1, s), jnp.int32(0))

                @pl.when(seen == 0)
                def _():
                    to_device(d, group, placed, 1).start()

                return placed + 1 - seen

            placed = lax.fori_loop(0, slots, slot, jnp.int32(0))

            def fill(j, carry):
                to_device(d, table[d, 0], j, 1).start()
                return carry

            lax.fori_loop(placed, span, fill, 0)

        def send(d, carry):
            @pl.when(starts[d] >= 0)
            def _():
                to_device(d, starts[d], 0, span).start()

            @pl.when(starts[d] < 0)
            def _():
                one_by_one(d)

            return carry

        lax.fori_loop(0, devices, send, 0)

    for d in range(devices):
        to_device(d, 0, 0, span).wait()


def pack(blocks_of, slopes, pieces=1):
    steps, samp_dev, width = slopes.shape
    devices, slots = blocks_of.shape
    tall = steps * samp_dev
    window = DISTINCT * BLOCK
    return pl.pallas_call(
        functools.partial(pack_kernel, pieces),
        out_shape=pltpu.HBM((devices, tall, window), slopes.dtype),
        in_specs=[pl.BlockSpec(memory_space=pltpu.HBM)] * 2,
        out_specs=pl.BlockSpec(memory_space=pltpu.HBM),
        scratch_shapes=[
            pltpu.VMEM((devices, slots), jnp.int32),
            pltpu.VMEM((tall, width + window), slopes.dtype),
            pltpu.SMEM((devices,), jnp.int32),
            pltpu.SMEM((devices, slots), jnp.int32),
            pltpu.SemaphoreType.DMA((devices,)),
            pltpu.SemaphoreType.DMA((pieces + 1, steps)),
            pltpu.SemaphoreType.DMA((2,)),
        ],
        compiler_params=pltpu.CompilerParams(vmem_limit_bytes=16 * MIB),
        name="pack_windows",
    )(pltpu.with_memory_space_constraint(blocks_of, pltpu.HBM), pltpu.with_memory_space_constraint(slopes, pltpu.HBM))


def plan_kernel(
    groups, blocks, slope_tab, act_tab, count_tab, weights,
    holder_out, kept,
    slopes, acts, counts, places, holder, table_sems, kept_sems, holder_sem,
):
    slots = weights.shape[0]
    loads = [
        pltpu.make_async_copy(source, held, table_sems.at[i])
        for i, (source, held) in enumerate(((slope_tab, slopes), (act_tab, acts), (count_tab, counts)))
    ]
    for load in loads:
        load.start()
    for load in loads:
        load.wait()
    own = lax.axis_index("samp")
    count = counts[0, own]
    half = groups // 2

    def turn(group):
        return jnp.where(group >= groups - half, group - (groups - half), group + half)

    def extent(k, spans):
        low_end, high_end, low_turned, high_turned = spans
        group = slopes[own, k]
        turned = turn(group)
        return (
            jnp.minimum(low_end, group), jnp.maximum(high_end, group),
            jnp.minimum(low_turned, turned), jnp.maximum(high_turned, turned),
        )

    first = slopes[own, 0]
    low_end, high_end, low_turned, high_turned = lax.fori_loop(
        1, slots, extent, (first, first, turn(first), turn(first))
    )
    straight = high_end - low_end < DISTINCT
    around = high_turned - low_turned < DISTINCT

    def clear(j, carry):
        holder[0, j] = jnp.int32(-1)
        return carry

    lax.fori_loop(0, holder.shape[1], clear, 0)

    def rank(k, placed):
        group = slopes[own, k]
        found = lax.fori_loop(0, k, lambda j, at: jnp.where(slopes[own, j] == group, places[j], at), jnp.int32(-1))
        places[k] = jnp.where(found >= 0, found, placed)
        return jnp.where(found >= 0, placed, placed + 1)

    @pl.when(jnp.logical_not(jnp.logical_or(straight, around)))
    def _():
        lax.fori_loop(0, slots, rank, jnp.int32(0))

    @pl.when(jnp.logical_or(straight, around))
    def _():
        def offset(k, carry):
            group = slopes[own, k]
            places[k] = jnp.where(straight, group - low_end, turn(group) - low_turned)
            return carry

        lax.fori_loop(0, slots, offset, 0)

    def keep(k):
        return pltpu.make_async_copy(weights.at[k], kept.at[k], kept_sems.at[k])

    def start_keep(k, carry):
        keep(k).start()
        return carry

    def wait_keep(k, carry):
        keep(k).wait()
        return carry

    lax.fori_loop(count, slots, start_keep, 0)

    def lay(k, carry):
        holder[0, places[k] * blocks + acts[own, k]] = k
        return carry

    lax.fori_loop(0, count, lay, 0)
    store = pltpu.make_async_copy(holder, holder_out, holder_sem)
    store.start()
    store.wait()
    lax.fori_loop(count, slots, wait_keep, 0)


def plan(groups, blocks, slope_tab, act_tab, count_tab, weights):
    slots = weights.shape[0]
    vmem = pl.BlockSpec(memory_space=pltpu.VMEM)
    hbm = pl.BlockSpec(memory_space=pltpu.HBM)
    return pl.pallas_call(
        functools.partial(plan_kernel, groups, blocks),
        out_shape=[pltpu.VMEM((1, BLOCK), jnp.int32), pltpu.HBM(weights.shape, jnp.float32)],
        in_specs=[hbm, hbm, hbm, vmem],
        out_specs=[vmem, hbm],
        scratch_shapes=[
            pltpu.SMEM(slope_tab.shape, jnp.int32),
            pltpu.SMEM(act_tab.shape, jnp.int32),
            pltpu.SMEM(count_tab.shape, jnp.int32),
            pltpu.SMEM((slots,), jnp.int32),
            pltpu.SMEM((1, BLOCK), jnp.int32),
            pltpu.SemaphoreType.DMA((3,)),
            pltpu.SemaphoreType.DMA((slots,)),
            pltpu.SemaphoreType.DMA,
        ],
        compiler_params=pltpu.CompilerParams(vmem_limit_bytes=16 * MIB),
        cost_estimate=pl.CostEstimate(flops=10**6, bytes_accessed=4 * 10**6, transcendentals=0),
        name="plan_cells",
    )(
        pltpu.with_memory_space_constraint(slope_tab, pltpu.HBM),
        pltpu.with_memory_space_constraint(act_tab, pltpu.HBM),
        pltpu.with_memory_space_constraint(count_tab, pltpu.HBM),
        weights,
    )


def spreader(samples, wide, samp_dev, step, dtype):
    tall = wide * samp_dev // samples
    n = lax.broadcasted_iota(jnp.int32, (samples, wide), 0)
    c = lax.broadcasted_iota(jnp.int32, (samples, wide), 1)
    column = (n // samp_dev) * tall + step * samp_dev + n % samp_dev
    return (c == column).astype(jnp.float32).astype(dtype)


def fit_kernel(
    step_rate, samp_dev, holder, seen, weights, targets, kept,
    fitted, residual, seen_turned, stack, low, rest_low, out_sems, rest_sem,
):
    steps, rows, samples = targets.shape
    count, block, _ = stack.shape
    wide, window = seen.shape
    span = window // block
    blocks = rows // block
    tall = wide * samp_dev // samples
    chunk = 2
    edges = list(range(0, span, chunk)) + [span]
    slot_of = [holder[0, j] for j in range(count)]

    def at_rows(a):
        return slice(a * block, (a + 1) * block)

    def at_cols(p):
        return slice(p * block, (p + 1) * block)

    def held(p, a):
        slot = slot_of[p * blocks + a]
        return jnp.where(slot >= 0, weights[jnp.maximum(slot, 0)], 0.0)

    def put(j, slot):
        return pltpu.make_async_copy(stack.at[j], fitted.at[slot], out_sems.at[j])

    for first, last in zip(edges, edges[1:]):
        at = slice(first * block, last * block)
        seen_turned[at, :] = seen[:, at].T
        for p in range(first, last):
            for a in range(blocks):
                low[at_rows(a), at_cols(p)] = held(p, a).astype(low.dtype)

    picks = [spreader(samples, wide, samp_dev, t, jnp.bfloat16) for t in range(steps)]
    wanted = [jnp.dot(targets[t], picks[t], preferred_element_type=jnp.float32) for t in range(steps)]
    column = lax.broadcasted_iota(jnp.int32, (block, wide), 1)
    step_of = (column % tall) // samp_dev
    store_rest = pltpu.make_async_copy(rest_low, residual, rest_sem)
    rests = [jnp.zeros((block, wide), jnp.bfloat16)] * blocks
    for t in range(steps):
        for a in range(blocks):
            predicted = jnp.dot(low[at_rows(a), :], seen_turned[...], preferred_element_type=jnp.float32)
            rest = (predicted - wanted[t][at_rows(a)]).astype(jnp.bfloat16)
            rests[a] = jnp.where(step_of == t, rest, rests[a])
        both = jnp.concatenate(rests, axis=0)
        if t == steps - 1:
            rest_low[...] = lax.dot_general(
                both, picks[t], (((1,), (1,)), ((), ())), preferred_element_type=jnp.float32
            ).astype(rest_low.dtype)
            store_rest.start()
        for first, last in zip(edges, edges[1:]):
            gradient = jnp.dot(both, seen[:, first * block : last * block], preferred_element_type=jnp.float32)
            pairs = [(p, a) for p in range(first, last) for a in range(blocks)]
            for p, a in pairs:
                j = p * blocks + a
                new = held(p, a) - step_rate * gradient[at_rows(a), at_cols(p - first)]
                if t < steps - 1:
                    low[at_rows(a), at_cols(p)] = jnp.where(slot_of[j] >= 0, new, 0.0).astype(low.dtype)
                else:
                    stack[j] = new
            if t == steps - 1:
                for p, a in pairs:

                    @pl.when(slot_of[p * blocks + a] >= 0)
                    def _(j=p * blocks + a):
                        put(j, slot_of[j]).start()

    store_rest.wait()
    for j in range(count):

        @pl.when(slot_of[j] >= 0)
        def _(j=j):
            put(j, 0).wait()


def fit(step_rate, samp_dev, holder, seen, weights, targets, kept):
    steps, rows, samples = targets.shape
    slots, block, _ = weights.shape
    wide, window = seen.shape
    count = rows // block * DISTINCT
    vmem = pl.BlockSpec(memory_space=pltpu.VMEM)
    hbm = pl.BlockSpec(memory_space=pltpu.HBM)
    return pl.pallas_call(
        functools.partial(fit_kernel, step_rate, samp_dev),
        out_shape=[
            pltpu.HBM(kept.shape, jnp.float32),
            pltpu.HBM((rows, samples), jnp.bfloat16),
        ],
        in_specs=[vmem, vmem, vmem, vmem, hbm],
        out_specs=[hbm, hbm],
        input_output_aliases={4: 0},
        scratch_shapes=[
            pltpu.VMEM((window, wide), seen.dtype),
            pltpu.VMEM((count, block, block), jnp.float32),
            pltpu.VMEM((rows, window), jnp.bfloat16),
            pltpu.VMEM((rows, samples), jnp.bfloat16),
            pltpu.SemaphoreType.DMA((count,)),
            pltpu.SemaphoreType.DMA,
        ],
        compiler_params=pltpu.CompilerParams(vmem_limit_bytes=24 * MIB),
        name="fit_steps",
    )(pltpu.with_memory_space_constraint(holder, pltpu.VMEM), seen, weights, targets, kept)


def fit_over_groups(step_rate, samp_dev, places, acts, arrived, weights, targets):
    steps, rows, samples = targets.shape
    slots, block, _ = weights.shape
    live = places >= 0
    devices = arrived.shape[0]
    grouped = arrived.reshape(devices, steps, samp_dev, DISTINCT, block)
    slot_slopes = jnp.take(grouped, jnp.maximum(places, 0), axis=3)
    blocks = rows // block
    onehot = ((acts[None, :] == jnp.arange(blocks)[:, None]) & live[None, :]).astype(jnp.float32)
    residual = None
    for t in range(steps):
        now = slot_slopes[:, t].reshape(samples, slots, block)
        partial_sums = jnp.einsum(
            "kil,nkl->kin", weights.astype(jnp.bfloat16), now, preferred_element_type=jnp.float32
        )
        summed = jnp.einsum("jk,kin->jin", onehot, partial_sums, precision=lax.Precision.HIGHEST)
        total = lax.psum(summed, "sens")
        residual = (total - targets[t].reshape(blocks, block, samples)).astype(jnp.bfloat16)
        gradient = jnp.einsum(
            "kin,nkl->kil", jnp.take(residual, acts, axis=0), now, preferred_element_type=jnp.float32
        )
        weights = jnp.where(live[:, None, None], weights - step_rate * gradient, weights)
    return weights, residual.reshape(rows, samples)


def per_device(slopes, targets, reconstructor, foot_act, foot_slope, foot_count):
    block = reconstructor.shape[-1]
    slots = reconstructor.shape[2]
    groups = slopes.shape[2] // block
    samp_dev = slopes.shape[1]
    samples = targets.shape[2]
    devices = foot_slope.shape[1]
    step_rate = slots * block / (samples + 3 * slots * block)
    packed = pack(foot_slope[0], slopes)
    arrived = lax.all_to_all(packed, "samp", split_axis=0, concat_axis=0, tiled=True)
    weights = reconstructor[0, 0]
    if lax.axis_size("sens") > 1:
        own_index = lax.axis_index("samp")

        def own(table):
            return lax.dynamic_index_in_dim(table, own_index, 0, keepdims=False)

        places = own_places(own(foot_slope[0]), own(foot_count[0]), groups)
        fitted, residual = fit_over_groups(
            step_rate, samp_dev, places, own(foot_act[0]), arrived, weights, targets
        )
        return fitted[None, None], residual
    blocks = targets.shape[1] // block
    holder, kept = plan(groups, blocks, foot_slope[0], foot_act[0], foot_count, weights)
    seen = arrived.reshape(devices * STEPS * samp_dev, DISTINCT * block)
    fitted, residual = fit(step_rate, samp_dev, holder, seen, weights, targets, kept)
    return fitted[None, None], residual


def solution(mesh):
    return jax.shard_map(
        per_device,
        mesh=mesh,
        in_specs=(
            P(None, "samp", "sens"),
            P(None, "samp", None),
            P("sens", "samp", None, None, None),
            P("sens", None, None),
            P("sens", None, None),
            P("sens", None),
        ),
        out_specs=(P("sens", "samp", None, None, None), P("samp", None)),
        check_vma=False,
    )
```

```python
import functools

import jax
import jax.numpy as jnp
from jax import lax
from jax.experimental import pallas as pl
from jax.experimental.pallas import tpu as pltpu
from jax.sharding import PartitionSpec as P

STEPS = 2
DISTINCT = 20
BLOCK = 128
MIB = 1 << 20


def own_places(blocks_own, count_own, groups):
    ids = jnp.arange(blocks_own.shape[0])
    half = groups // 2
    turned = jnp.where(blocks_own >= groups - half, blocks_own - (groups - half), blocks_own + half)
    straight = blocks_own - jnp.min(blocks_own)
    around = turned - jnp.min(turned)
    same = blocks_own[:, None] == blocks_own[None, :]
    before = ids[None, :] < ids[:, None]
    first = ~jnp.any(same & before, axis=1)
    rank = jnp.sum(first[None, :] & before, axis=1)
    ranked = jnp.sum(jnp.where(same & first[None, :], rank[None, :], 0), axis=1)
    place = jnp.where(
        jnp.max(straight) < DISTINCT, straight, jnp.where(jnp.max(around) < DISTINCT, around, ranked)
    )
    return jnp.where(ids < count_own, place, -1).astype(jnp.int32)


def pack_kernel(pieces, blocks_hbm, slopes, out, blocks_of, rows, starts, table, sems, load_sems, table_sems):
    steps, samp_dev, width = slopes.shape
    groups = width // BLOCK
    devices, _, window = out.shape
    span = window // BLOCK
    slots = blocks_of.shape[1]
    half = groups // 2

    read_table = pltpu.make_async_copy(blocks_hbm, blocks_of, table_sems.at[0])
    read_table.start()
    parts = [(groups * i // pieces, groups * (i + 1) // pieces, 0) for i in range(pieces)] + [(0, span, groups)]
    loads = []
    for i, (first, last, shift) in enumerate(parts):
        for t in range(steps):
            source = slopes.at[t, :, pl.ds(first * BLOCK, (last - first) * BLOCK)]
            target = rows.at[pl.ds(t * samp_dev, samp_dev), pl.ds((first + shift) * BLOCK, (last - first) * BLOCK)]
            loads.append(pltpu.make_async_copy(source, target, load_sems.at[i, t]))
    for load in loads:
        load.start()

    read_table.wait()
    blocks = blocks_of[...].astype(jnp.float32)
    turned = jnp.where(blocks >= groups - half, blocks - (groups - half), blocks + half)

    def extent(named):
        low = jnp.min(named, axis=1, keepdims=True)
        return low, jnp.max(named, axis=1, keepdims=True) - low < DISTINCT

    low, fits = extent(blocks)
    low_turned, fits_turned = extent(turned)
    unturned = jnp.where(low_turned >= half, low_turned - half, low_turned + (groups - half))
    first = jnp.where(fits, low, jnp.where(fits_turned, unturned, -1.0)).astype(jnp.int32)
    first_of = [first[d, 0] for d in range(devices)]
    least = functools.reduce(jnp.minimum, first_of)
    for load in loads:
        load.wait()

    def to_device(d, group, at, count):
        return pltpu.make_async_copy(
            rows.at[:, pl.ds(pl.multiple_of(group * BLOCK, BLOCK), count * BLOCK)],
            out.at[d, :, pl.ds(pl.multiple_of(at * BLOCK, BLOCK), count * BLOCK)],
            sems.at[d],
        )

    @pl.when(least >= 0)
    def _():
        for d in range(devices):
            to_device(d, first_of[d], 0, span).start()

    @pl.when(least < 0)
    def _():
        for d in range(devices):
            starts[d] = first_of[d]
        copy_table = pltpu.make_async_copy(blocks_of, table, table_sems.at[1])
        copy_table.start()
        copy_table.wait()

        def one_by_one(d):
            def slot(k, placed):
                group = table[d, k]
                seen = lax.fori_loop(0, k, lambda j, s: jnp.where(table[d, j] == group, 1, s), jnp.int32(0))

                @pl.when(seen == 0)
                def _():
                    to_device(d, group, placed, 1).start()

                return placed + 1 - seen

            placed = lax.fori_loop(0, slots, slot, jnp.int32(0))

            def fill(j, carry):
                to_device(d, table[d, 0], j, 1).start()
                return carry

            lax.fori_loop(placed, span, fill, 0)

        def send(d, carry):
            @pl.when(starts[d] >= 0)
            def _():
                to_device(d, starts[d], 0, span).start()

            @pl.when(starts[d] < 0)
            def _():
                one_by_one(d)

            return carry

        lax.fori_loop(0, devices, send, 0)

    for d in range(devices):
        to_device(d, 0, 0, span).wait()


def pack(blocks_of, slopes, pieces=1):
    steps, samp_dev, width = slopes.shape
    devices, slots = blocks_of.shape
    tall = steps * samp_dev
    window = DISTINCT * BLOCK
    return pl.pallas_call(
        functools.partial(pack_kernel, pieces),
        out_shape=pltpu.HBM((devices, tall, window), slopes.dtype),
        in_specs=[pl.BlockSpec(memory_space=pltpu.HBM)] * 2,
        out_specs=pl.BlockSpec(memory_space=pltpu.HBM),
        scratch_shapes=[
            pltpu.VMEM((devices, slots), jnp.int32),
            pltpu.VMEM((tall, width + window), slopes.dtype),
            pltpu.SMEM((devices,), jnp.int32),
            pltpu.SMEM((devices, slots), jnp.int32),
            pltpu.SemaphoreType.DMA((devices,)),
            pltpu.SemaphoreType.DMA((pieces + 1, steps)),
            pltpu.SemaphoreType.DMA((2,)),
        ],
        compiler_params=pltpu.CompilerParams(vmem_limit_bytes=16 * MIB),
        name="pack_windows",
    )(pltpu.with_memory_space_constraint(blocks_of, pltpu.HBM), pltpu.with_memory_space_constraint(slopes, pltpu.HBM))


def plan_kernel(
    groups, blocks, slope_tab, act_tab, count_tab, weights,
    holder_out, kept,
    slopes, acts, counts, places, holder, table_sems, kept_sems, holder_sem,
):
    slots = weights.shape[0]
    loads = [
        pltpu.make_async_copy(source, held, table_sems.at[i])
        for i, (source, held) in enumerate(((slope_tab, slopes), (act_tab, acts), (count_tab, counts)))
    ]
    for load in loads:
        load.start()
    for load in loads:
        load.wait()
    own = lax.axis_index("samp")
    count = counts[0, own]
    half = groups // 2

    def turn(group):
        return jnp.where(group >= groups - half, group - (groups - half), group + half)

    def extent(k, spans):
        low_end, high_end, low_turned, high_turned = spans
        group = slopes[own, k]
        turned = turn(group)
        return (
            jnp.minimum(low_end, group), jnp.maximum(high_end, group),
            jnp.minimum(low_turned, turned), jnp.maximum(high_turned, turned),
        )

    first = slopes[own, 0]
    low_end, high_end, low_turned, high_turned = lax.fori_loop(
        1, slots, extent, (first, first, turn(first), turn(first))
    )
    straight = high_end - low_end < DISTINCT
    around = high_turned - low_turned < DISTINCT

    def clear(j, carry):
        holder[0, j] = jnp.int32(-1)
        return carry

    lax.fori_loop(0, holder.shape[1], clear, 0)

    def rank(k, placed):
        group = slopes[own, k]
        found = lax.fori_loop(0, k, lambda j, at: jnp.where(slopes[own, j] == group, places[j], at), jnp.int32(-1))
        places[k] = jnp.where(found >= 0, found, placed)
        return jnp.where(found >= 0, placed, placed + 1)

    @pl.when(jnp.logical_not(jnp.logical_or(straight, around)))
    def _():
        lax.fori_loop(0, slots, rank, jnp.int32(0))

    @pl.when(jnp.logical_or(straight, around))
    def _():
        def offset(k, carry):
            group = slopes[own, k]
            places[k] = jnp.where(straight, group - low_end, turn(group) - low_turned)
            return carry

        lax.fori_loop(0, slots, offset, 0)

    def keep(k):
        return pltpu.make_async_copy(weights.at[k], kept.at[k], kept_sems.at[k])

    def start_keep(k, carry):
        keep(k).start()
        return carry

    def wait_keep(k, carry):
        keep(k).wait()
        return carry

    lax.fori_loop(count, slots, start_keep, 0)

    def lay(k, carry):
        holder[0, places[k] * blocks + acts[own, k]] = k
        return carry

    lax.fori_loop(0, count, lay, 0)
    store = pltpu.make_async_copy(holder, holder_out, holder_sem)
    store.start()
    store.wait()
    lax.fori_loop(count, slots, wait_keep, 0)


def plan(groups, blocks, slope_tab, act_tab, count_tab, weights):
    slots = weights.shape[0]
    vmem = pl.BlockSpec(memory_space=pltpu.VMEM)
    hbm = pl.BlockSpec(memory_space=pltpu.HBM)
    return pl.pallas_call(
        functools.partial(plan_kernel, groups, blocks),
        out_shape=[pltpu.VMEM((1, BLOCK), jnp.int32), pltpu.HBM(weights.shape, jnp.float32)],
        in_specs=[hbm, hbm, hbm, vmem],
        out_specs=[vmem, hbm],
        scratch_shapes=[
            pltpu.SMEM(slope_tab.shape, jnp.int32),
            pltpu.SMEM(act_tab.shape, jnp.int32),
            pltpu.SMEM(count_tab.shape, jnp.int32),
            pltpu.SMEM((slots,), jnp.int32),
            pltpu.SMEM((1, BLOCK), jnp.int32),
            pltpu.SemaphoreType.DMA((3,)),
            pltpu.SemaphoreType.DMA((slots,)),
            pltpu.SemaphoreType.DMA,
        ],
        compiler_params=pltpu.CompilerParams(vmem_limit_bytes=16 * MIB),
        cost_estimate=pl.CostEstimate(flops=10**6, bytes_accessed=4 * 10**6, transcendentals=0),
        name="plan_cells",
    )(
        pltpu.with_memory_space_constraint(slope_tab, pltpu.HBM),
        pltpu.with_memory_space_constraint(act_tab, pltpu.HBM),
        pltpu.with_memory_space_constraint(count_tab, pltpu.HBM),
        weights,
    )


def mixer(shape, samples, samp_dev, order, dtype):
    steps = shape[0] // samples
    tall = steps * samp_dev
    line = lax.broadcasted_iota(jnp.int32, (1, shape[1]), 1)
    turn, inner = line // tall, line % tall
    source = turn
    if order != tuple(range(len(order))):
        source = functools.reduce(jnp.add, [jnp.where(turn == r, d, 0) for r, d in enumerate(order)])
    row = (inner // samp_dev) * samples + source * samp_dev + inner % samp_dev
    return (lax.broadcasted_iota(jnp.int32, shape, 0) == row).astype(jnp.float32).astype(dtype), inner // samp_dev


def fit_kernel(
    step_rate, samp_dev, order, holder, seen, weights, targets, kept,
    fitted, residual, stack, rest_low, out_sems, rest_sem, *sums,
):
    steps, rows, samples = targets.shape
    count, block, _ = stack.shape
    wide, window = seen.shape
    blocks = rows // block
    pair = wide // block
    tiles = window // wide
    slot_of = [holder[0, j] for j in range(count)]

    def region(tile, part):
        return sums[part * 2 + tile % 2]

    def cell(tile, q, a):
        return (tile * pair + q) * blocks + a

    def held(j):
        slot = slot_of[j]
        return jnp.where(slot >= 0, weights[jnp.maximum(slot, 0)], 0.0)

    def join(parts):
        return jnp.concatenate([jnp.concatenate(line, axis=1) for line in parts], axis=0)

    def multiply(tile, lhs, rhs, part, transpose=False):
        stage = (tile // 2) % 2
        pltpu.matmul_push_rhs(rhs, stage, tile % 2, transpose=transpose)
        pltpu.matmul_acc_lhs(region(tile, part), lhs, load_staged_rhs=stage)

    def tile_of(tile):
        return seen[:, tile * wide : (tile + 1) * wide]

    mix, step_of = mixer((steps * samples, wide), samples, samp_dev, order, jnp.bfloat16)
    for tile in range(tiles):
        start = join([[held(cell(tile, q, a)) for q in range(pair)] for a in range(blocks)]).astype(jnp.bfloat16)
        multiply(tile, start, tile_of(tile), 0, transpose=True)
    multiply(0, jnp.concatenate([targets[t] for t in range(steps)], axis=1), mix, 1)
    wanted = pltpu.matmul_pop(region(0, 1))
    store_rest = pltpu.make_async_copy(rest_low, residual, rest_sem)
    both = jnp.zeros((rows, wide), jnp.bfloat16)
    for t in range(steps):
        predicted = pltpu.matmul_pop(region(0, 0)) + pltpu.matmul_pop(region(1, 0))
        both = jnp.where(step_of == t, (predicted - wanted).astype(jnp.bfloat16), both)
        if t == steps - 1:
            multiply(0, both, mix, 0, transpose=True)
            last = pltpu.matmul_pop(region(0, 0))
            rest_low[...] = last[:, t * samples : (t + 1) * samples].astype(rest_low.dtype)
            store_rest.start()
        multiply(0, both, tile_of(0), 1)
        multiply(1, both, tile_of(1), 1)
        for tile in range(tiles):
            gradient = pltpu.matmul_pop(region(tile, 1 + (tile // 2) % 2))
            if tile + 2 < tiles:
                multiply(tile + 2, both, tile_of(tile + 2), 1 + (tile // 2 + 1) % 2)
            parts = []
            for a in range(blocks):
                line = []
                for q in range(pair):
                    j = cell(tile, q, a)
                    moved = gradient[a * block : (a + 1) * block, q * block : (q + 1) * block]
                    new = held(j) - step_rate * moved
                    if t < steps - 1:
                        line.append(jnp.where(slot_of[j] >= 0, new, 0.0))
                    else:
                        stack[j] = new
                parts.append(line)
            if t < steps - 1:
                multiply(tile, join(parts).astype(jnp.bfloat16), tile_of(tile), 0, transpose=True)
            else:
                for a in range(blocks):
                    for q in range(pair):
                        j = cell(tile, q, a)

                        @pl.when(slot_of[j] >= 0)
                        def _(j=j):
                            pltpu.make_async_copy(stack.at[j], fitted.at[slot_of[j]], out_sems.at[j]).start()

    store_rest.wait()
    for j in range(count):

        @pl.when(slot_of[j] >= 0)
        def _(j=j):
            pltpu.make_async_copy(stack.at[j], fitted.at[0], out_sems.at[j]).wait()


def fit(step_rate, samp_dev, order, holder, seen, weights, targets, kept):
    steps, rows, samples = targets.shape
    slots, block, _ = weights.shape
    wide, window = seen.shape
    count = rows // block * DISTINCT
    vmem = pl.BlockSpec(memory_space=pltpu.VMEM)
    hbm = pl.BlockSpec(memory_space=pltpu.HBM)

    def kernel(*refs):
        pl.run_scoped(
            functools.partial(fit_kernel, step_rate, samp_dev, order, *refs),
            *[pltpu.ACC(unit)((rows, wide), jnp.float32) for part in range(3) for unit in range(2)],
        )

    return pl.pallas_call(
        kernel,
        out_shape=[
            pltpu.HBM(kept.shape, jnp.float32),
            pltpu.HBM((rows, samples), jnp.bfloat16),
        ],
        in_specs=[vmem, vmem, vmem, vmem, hbm],
        out_specs=[hbm, hbm],
        input_output_aliases={4: 0},
        scratch_shapes=[
            pltpu.VMEM((count, block, block), jnp.float32),
            pltpu.VMEM((rows, samples), jnp.bfloat16),
            pltpu.SemaphoreType.DMA((count,)),
            pltpu.SemaphoreType.DMA,
        ],
        compiler_params=pltpu.CompilerParams(vmem_limit_bytes=24 * MIB),
        name="fit_steps",
    )(pltpu.with_memory_space_constraint(holder, pltpu.VMEM), seen, weights, targets, kept)


def fit_over_groups(step_rate, samp_dev, places, acts, arrived, weights, targets):
    steps, rows, samples = targets.shape
    slots, block, _ = weights.shape
    live = places >= 0
    devices = arrived.shape[0]
    grouped = arrived.reshape(devices, steps, samp_dev, DISTINCT, block)
    slot_slopes = jnp.take(grouped, jnp.maximum(places, 0), axis=3)
    blocks = rows // block
    onehot = ((acts[None, :] == jnp.arange(blocks)[:, None]) & live[None, :]).astype(jnp.float32)
    residual = None
    for t in range(steps):
        now = slot_slopes[:, t].reshape(samples, slots, block)
        partial_sums = jnp.einsum(
            "kil,nkl->kin", weights.astype(jnp.bfloat16), now, preferred_element_type=jnp.float32
        )
        summed = jnp.einsum("jk,kin->jin", onehot, partial_sums, precision=lax.Precision.HIGHEST)
        total = lax.psum(summed, "sens")
        residual = (total - targets[t].reshape(blocks, block, samples)).astype(jnp.bfloat16)
        gradient = jnp.einsum(
            "kin,nkl->kil", jnp.take(residual, acts, axis=0), now, preferred_element_type=jnp.float32
        )
        weights = jnp.where(live[:, None, None], weights - step_rate * gradient, weights)
    return weights, residual.reshape(rows, samples)


def per_device(slopes, targets, reconstructor, foot_act, foot_slope, foot_count):
    block = reconstructor.shape[-1]
    slots = reconstructor.shape[2]
    groups = slopes.shape[2] // block
    samp_dev = slopes.shape[1]
    samples = targets.shape[2]
    devices = foot_slope.shape[1]
    step_rate = slots * block / (samples + 3 * slots * block)
    order = tuple(range(devices))
    packed = pack(foot_slope[0], slopes)
    arrived = lax.all_to_all(packed, "samp", split_axis=0, concat_axis=0, tiled=True)
    weights = reconstructor[0, 0]
    if lax.axis_size("sens") > 1:
        own_index = lax.axis_index("samp")

        def own(table):
            return lax.dynamic_index_in_dim(table, own_index, 0, keepdims=False)

        places = own_places(own(foot_slope[0]), own(foot_count[0]), groups)
        fitted, residual = fit_over_groups(
            step_rate, samp_dev, places, own(foot_act[0]), arrived, weights, targets
        )
        return fitted[None, None], residual
    blocks = targets.shape[1] // block
    holder, kept = plan(groups, blocks, foot_slope[0], foot_act[0], foot_count, weights)
    seen = arrived.reshape(devices * STEPS * samp_dev, DISTINCT * block)
    fitted, residual = fit(step_rate, samp_dev, order, holder, seen, weights, targets, kept)
    return fitted[None, None], residual


def solution(mesh):
    return jax.shard_map(
        per_device,
        mesh=mesh,
        in_specs=(
            P(None, "samp", "sens"),
            P(None, "samp", None),
            P("sens", "samp", None, None, None),
            P("sens", None, None),
            P("sens", None, None),
            P("sens", None),
        ),
        out_specs=(P("sens", "samp", None, None, None), P("samp", None)),
        check_vma=False,
    )
```

```python
import functools

import jax
import jax.numpy as jnp
from jax import lax
from jax.experimental import pallas as pl
from jax.experimental.pallas import tpu as pltpu
from jax.sharding import PartitionSpec as P

STEPS = 2
DISTINCT = 20
BLOCK = 128
ORDERS = {
    32: (24, 7, 25, 12, 31, 29, 3, 19, 21, 4, 18, 10, 28, 20, 5, 23, 16, 9, 14, 13, 11, 27, 6, 2, 22, 1, 15, 26, 8, 17, 0, 30),
}
MIB = 1 << 20


def own_places(blocks_own, count_own, groups):
    ids = jnp.arange(blocks_own.shape[0])
    half = groups // 2
    turned = jnp.where(blocks_own >= groups - half, blocks_own - (groups - half), blocks_own + half)
    straight = blocks_own - jnp.min(blocks_own)
    around = turned - jnp.min(turned)
    same = blocks_own[:, None] == blocks_own[None, :]
    before = ids[None, :] < ids[:, None]
    first = ~jnp.any(same & before, axis=1)
    rank = jnp.sum(first[None, :] & before, axis=1)
    ranked = jnp.sum(jnp.where(same & first[None, :], rank[None, :], 0), axis=1)
    place = jnp.where(
        jnp.max(straight) < DISTINCT, straight, jnp.where(jnp.max(around) < DISTINCT, around, ranked)
    )
    return jnp.where(ids < count_own, place, -1).astype(jnp.int32)


def pack_kernel(
    pieces, order, blocks_hbm, slopes, out, blocks_of, rows, starts, turns, table, sems, load_sems, table_sems
):
    steps, samp_dev, width = slopes.shape
    groups = width // BLOCK
    devices, _, window = out.shape
    span = window // BLOCK
    slots = blocks_of.shape[1]
    half = groups // 2

    read_table = pltpu.make_async_copy(blocks_hbm, blocks_of, table_sems.at[0])
    read_table.start()
    parts = [(groups * i // pieces, groups * (i + 1) // pieces, 0) for i in range(pieces)] + [(0, span, groups)]
    loads = []
    for i, (first, last, shift) in enumerate(parts):
        for t in range(steps):
            source = slopes.at[t, :, pl.ds(first * BLOCK, (last - first) * BLOCK)]
            target = rows.at[pl.ds(t * samp_dev, samp_dev), pl.ds((first + shift) * BLOCK, (last - first) * BLOCK)]
            loads.append(pltpu.make_async_copy(source, target, load_sems.at[i, t]))
    for load in loads:
        load.start()

    read_table.wait()
    blocks = blocks_of[...].astype(jnp.float32)
    turned = jnp.where(blocks >= groups - half, blocks - (groups - half), blocks + half)

    def extent(named):
        low = jnp.min(named, axis=1, keepdims=True)
        return low, jnp.max(named, axis=1, keepdims=True) - low < DISTINCT

    low, fits = extent(blocks)
    low_turned, fits_turned = extent(turned)
    unturned = jnp.where(low_turned >= half, low_turned - half, low_turned + (groups - half))
    first = jnp.where(fits, low, jnp.where(fits_turned, unturned, -1.0)).astype(jnp.int32)
    first_of = [first[d, 0] for d in range(devices)]
    least = functools.reduce(jnp.minimum, first_of)
    for load in loads:
        load.wait()

    def to_turn(r, group, at, count):
        return pltpu.make_async_copy(
            rows.at[:, pl.ds(pl.multiple_of(group * BLOCK, BLOCK), count * BLOCK)],
            out.at[r, :, pl.ds(pl.multiple_of(at * BLOCK, BLOCK), count * BLOCK)],
            sems.at[r],
        )

    @pl.when(least >= 0)
    def _():
        for r, d in enumerate(order):
            to_turn(r, first_of[d], 0, span).start()

    @pl.when(least < 0)
    def _():
        for r, d in enumerate(order):
            starts[r] = first_of[d]
            turns[r] = jnp.int32(d)
        copy_table = pltpu.make_async_copy(blocks_of, table, table_sems.at[1])
        copy_table.start()
        copy_table.wait()

        def one_by_one(r):
            d = turns[r]

            def slot(k, placed):
                group = table[d, k]
                seen = lax.fori_loop(0, k, lambda j, s: jnp.where(table[d, j] == group, 1, s), jnp.int32(0))

                @pl.when(seen == 0)
                def _():
                    to_turn(r, group, placed, 1).start()

                return placed + 1 - seen

            placed = lax.fori_loop(0, slots, slot, jnp.int32(0))

            def fill(j, carry):
                to_turn(r, table[d, 0], j, 1).start()
                return carry

            lax.fori_loop(placed, span, fill, 0)

        def send(r, carry):
            @pl.when(starts[r] >= 0)
            def _():
                to_turn(r, starts[r], 0, span).start()

            @pl.when(starts[r] < 0)
            def _():
                one_by_one(r)

            return carry

        lax.fori_loop(0, devices, send, 0)

    for r in range(devices):
        to_turn(r, 0, 0, span).wait()


def pack(order, blocks_of, slopes, pieces=1):
    steps, samp_dev, width = slopes.shape
    devices, slots = blocks_of.shape
    tall = steps * samp_dev
    window = DISTINCT * BLOCK
    return pl.pallas_call(
        functools.partial(pack_kernel, pieces, order),
        out_shape=pltpu.HBM((devices, tall, window), slopes.dtype),
        in_specs=[pl.BlockSpec(memory_space=pltpu.HBM)] * 2,
        out_specs=pl.BlockSpec(memory_space=pltpu.HBM),
        scratch_shapes=[
            pltpu.VMEM((devices, slots), jnp.int32),
            pltpu.VMEM((tall, width + window), slopes.dtype),
            pltpu.SMEM((devices,), jnp.int32),
            pltpu.SMEM((devices,), jnp.int32),
            pltpu.SMEM((devices, slots), jnp.int32),
            pltpu.SemaphoreType.DMA((devices,)),
            pltpu.SemaphoreType.DMA((pieces + 1, steps)),
            pltpu.SemaphoreType.DMA((2,)),
        ],
        compiler_params=pltpu.CompilerParams(vmem_limit_bytes=16 * MIB),
        name="pack_windows",
    )(pltpu.with_memory_space_constraint(blocks_of, pltpu.HBM), pltpu.with_memory_space_constraint(slopes, pltpu.HBM))


def plan_kernel(
    groups, blocks, slope_tab, act_tab, count_tab, weights,
    holder_out, kept,
    slopes, acts, counts, places, holder, table_sems, kept_sems, holder_sem,
):
    slots = weights.shape[0]
    loads = [
        pltpu.make_async_copy(source, held, table_sems.at[i])
        for i, (source, held) in enumerate(((slope_tab, slopes), (act_tab, acts), (count_tab, counts)))
    ]
    for load in loads:
        load.start()
    for load in loads:
        load.wait()
    own = lax.axis_index("samp")
    count = counts[0, own]
    half = groups // 2

    def turn(group):
        return jnp.where(group >= groups - half, group - (groups - half), group + half)

    def extent(k, spans):
        low_end, high_end, low_turned, high_turned = spans
        group = slopes[own, k]
        turned = turn(group)
        return (
            jnp.minimum(low_end, group), jnp.maximum(high_end, group),
            jnp.minimum(low_turned, turned), jnp.maximum(high_turned, turned),
        )

    first = slopes[own, 0]
    low_end, high_end, low_turned, high_turned = lax.fori_loop(
        1, slots, extent, (first, first, turn(first), turn(first))
    )
    straight = high_end - low_end < DISTINCT
    around = high_turned - low_turned < DISTINCT

    def clear(j, carry):
        holder[0, j] = jnp.int32(-1)
        return carry

    lax.fori_loop(0, holder.shape[1], clear, 0)

    def rank(k, placed):
        group = slopes[own, k]
        found = lax.fori_loop(0, k, lambda j, at: jnp.where(slopes[own, j] == group, places[j], at), jnp.int32(-1))
        places[k] = jnp.where(found >= 0, found, placed)
        return jnp.where(found >= 0, placed, placed + 1)

    @pl.when(jnp.logical_not(jnp.logical_or(straight, around)))
    def _():
        lax.fori_loop(0, slots, rank, jnp.int32(0))

    @pl.when(jnp.logical_or(straight, around))
    def _():
        def offset(k, carry):
            group = slopes[own, k]
            places[k] = jnp.where(straight, group - low_end, turn(group) - low_turned)
            return carry

        lax.fori_loop(0, slots, offset, 0)

    def keep(k):
        return pltpu.make_async_copy(weights.at[k], kept.at[k], kept_sems.at[k])

    def start_keep(k, carry):
        keep(k).start()
        return carry

    def wait_keep(k, carry):
        keep(k).wait()
        return carry

    lax.fori_loop(count, slots, start_keep, 0)

    def lay(k, carry):
        holder[0, places[k] * blocks + acts[own, k]] = k
        return carry

    lax.fori_loop(0, count, lay, 0)
    store = pltpu.make_async_copy(holder, holder_out, holder_sem)
    store.start()
    store.wait()
    lax.fori_loop(count, slots, wait_keep, 0)


def plan(groups, blocks, slope_tab, act_tab, count_tab, weights):
    slots = weights.shape[0]
    vmem = pl.BlockSpec(memory_space=pltpu.VMEM)
    hbm = pl.BlockSpec(memory_space=pltpu.HBM)
    return pl.pallas_call(
        functools.partial(plan_kernel, groups, blocks),
        out_shape=[pltpu.VMEM((1, BLOCK), jnp.int32), pltpu.HBM(weights.shape, jnp.float32)],
        in_specs=[hbm, hbm, hbm, vmem],
        out_specs=[vmem, hbm],
        scratch_shapes=[
            pltpu.SMEM(slope_tab.shape, jnp.int32),
            pltpu.SMEM(act_tab.shape, jnp.int32),
            pltpu.SMEM(count_tab.shape, jnp.int32),
            pltpu.SMEM((slots,), jnp.int32),
            pltpu.SMEM((1, BLOCK), jnp.int32),
            pltpu.SemaphoreType.DMA((3,)),
            pltpu.SemaphoreType.DMA((slots,)),
            pltpu.SemaphoreType.DMA,
        ],
        compiler_params=pltpu.CompilerParams(vmem_limit_bytes=16 * MIB),
        cost_estimate=pl.CostEstimate(flops=10**6, bytes_accessed=4 * 10**6, transcendentals=0),
        name="plan_cells",
    )(
        pltpu.with_memory_space_constraint(slope_tab, pltpu.HBM),
        pltpu.with_memory_space_constraint(act_tab, pltpu.HBM),
        pltpu.with_memory_space_constraint(count_tab, pltpu.HBM),
        weights,
    )


def mixer(shape, samples, samp_dev, order, dtype):
    steps = shape[0] // samples
    tall = steps * samp_dev
    line = lax.broadcasted_iota(jnp.int32, (1, shape[1]), 1)
    turn, inner = line // tall, line % tall
    source = turn
    if order != tuple(range(len(order))):
        source = functools.reduce(jnp.add, [jnp.where(turn == r, d, 0) for r, d in enumerate(order)])
    row = (inner // samp_dev) * samples + source * samp_dev + inner % samp_dev
    return (lax.broadcasted_iota(jnp.int32, shape, 0) == row).astype(jnp.float32).astype(dtype), inner // samp_dev


def fit_kernel(
    step_rate, samp_dev, order, holder, seen, weights, targets, kept,
    fitted, residual, stack, rest_low, out_sems, rest_sem, *sums,
):
    steps, rows, samples = targets.shape
    count, block, _ = stack.shape
    wide, window = seen.shape
    blocks = rows // block
    pair = wide // block
    tiles = window // wide
    slot_of = [holder[0, j] for j in range(count)]

    def region(tile, part):
        return sums[part * 2 + tile % 2]

    def cell(tile, q, a):
        return (tile * pair + q) * blocks + a

    def held(j):
        slot = slot_of[j]
        return jnp.where(slot >= 0, weights[jnp.maximum(slot, 0)], 0.0)

    def join(parts):
        return jnp.concatenate([jnp.concatenate(line, axis=1) for line in parts], axis=0)

    def multiply(tile, lhs, rhs, part, transpose=False):
        stage = (tile // 2) % 2
        pltpu.matmul_push_rhs(rhs, stage, tile % 2, transpose=transpose)
        pltpu.matmul_acc_lhs(region(tile, part), lhs, load_staged_rhs=stage)

    def tile_of(tile):
        return seen[:, tile * wide : (tile + 1) * wide]

    mix, step_of = mixer((steps * samples, wide), samples, samp_dev, order, jnp.bfloat16)
    for tile in range(tiles):
        start = join([[held(cell(tile, q, a)) for q in range(pair)] for a in range(blocks)]).astype(jnp.bfloat16)
        multiply(tile, start, tile_of(tile), 0, transpose=True)
    multiply(0, jnp.concatenate([targets[t] for t in range(steps)], axis=1), mix, 1)
    wanted = pltpu.matmul_pop(region(0, 1))
    store_rest = pltpu.make_async_copy(rest_low, residual, rest_sem)
    both = jnp.zeros((rows, wide), jnp.bfloat16)
    for t in range(steps):
        predicted = pltpu.matmul_pop(region(0, 0)) + pltpu.matmul_pop(region(1, 0))
        both = jnp.where(step_of == t, (predicted - wanted).astype(jnp.bfloat16), both)
        if t == steps - 1:
            multiply(0, both, mix, 0, transpose=True)
            last = pltpu.matmul_pop(region(0, 0))
            rest_low[...] = last[:, t * samples : (t + 1) * samples].astype(rest_low.dtype)
            store_rest.start()
        multiply(0, both, tile_of(0), 1)
        multiply(1, both, tile_of(1), 1)
        for tile in range(tiles):
            gradient = pltpu.matmul_pop(region(tile, 1 + (tile // 2) % 2))
            if tile + 2 < tiles:
                multiply(tile + 2, both, tile_of(tile + 2), 1 + (tile // 2 + 1) % 2)
            parts = []
            for a in range(blocks):
                line = []
                for q in range(pair):
                    j = cell(tile, q, a)
                    moved = gradient[a * block : (a + 1) * block, q * block : (q + 1) * block]
                    new = held(j) - step_rate * moved
                    if t < steps - 1:
                        line.append(jnp.where(slot_of[j] >= 0, new, 0.0))
                    else:
                        stack[j] = new
                parts.append(line)
            if t < steps - 1:
                multiply(tile, join(parts).astype(jnp.bfloat16), tile_of(tile), 0, transpose=True)
            else:
                for a in range(blocks):
                    for q in range(pair):
                        j = cell(tile, q, a)

                        @pl.when(slot_of[j] >= 0)
                        def _(j=j):
                            pltpu.make_async_copy(stack.at[j], fitted.at[slot_of[j]], out_sems.at[j]).start()

    store_rest.wait()
    for j in range(count):

        @pl.when(slot_of[j] >= 0)
        def _(j=j):
            pltpu.make_async_copy(stack.at[j], fitted.at[0], out_sems.at[j]).wait()


def fit(step_rate, samp_dev, order, holder, seen, weights, targets, kept):
    steps, rows, samples = targets.shape
    slots, block, _ = weights.shape
    wide, window = seen.shape
    count = rows // block * DISTINCT
    vmem = pl.BlockSpec(memory_space=pltpu.VMEM)
    hbm = pl.BlockSpec(memory_space=pltpu.HBM)

    def kernel(*refs):
        pl.run_scoped(
            functools.partial(fit_kernel, step_rate, samp_dev, order, *refs),
            *[pltpu.ACC(unit)((rows, wide), jnp.float32) for part in range(3) for unit in range(2)],
        )

    return pl.pallas_call(
        kernel,
        out_shape=[
            pltpu.HBM(kept.shape, jnp.float32),
            pltpu.HBM((rows, samples), jnp.bfloat16),
        ],
        in_specs=[vmem, vmem, vmem, vmem, hbm],
        out_specs=[hbm, hbm],
        input_output_aliases={4: 0},
        scratch_shapes=[
            pltpu.VMEM((count, block, block), jnp.float32),
            pltpu.VMEM((rows, samples), jnp.bfloat16),
            pltpu.SemaphoreType.DMA((count,)),
            pltpu.SemaphoreType.DMA,
        ],
        compiler_params=pltpu.CompilerParams(vmem_limit_bytes=24 * MIB),
        name="fit_steps",
    )(pltpu.with_memory_space_constraint(holder, pltpu.VMEM), seen, weights, targets, kept)


def fit_over_groups(step_rate, samp_dev, order, places, acts, arrived, weights, targets):
    steps, rows, samples = targets.shape
    slots, block, _ = weights.shape
    live = places >= 0
    devices = arrived.shape[0]
    if order != tuple(range(devices)):
        arrived = jnp.stack([arrived[order.index(d)] for d in range(devices)])
    grouped = arrived.reshape(devices, steps, samp_dev, DISTINCT, block)
    slot_slopes = jnp.take(grouped, jnp.maximum(places, 0), axis=3)
    blocks = rows // block
    onehot = ((acts[None, :] == jnp.arange(blocks)[:, None]) & live[None, :]).astype(jnp.float32)
    residual = None
    for t in range(steps):
        now = slot_slopes[:, t].reshape(samples, slots, block)
        partial_sums = jnp.einsum(
            "kil,nkl->kin", weights.astype(jnp.bfloat16), now, preferred_element_type=jnp.float32
        )
        summed = jnp.einsum("jk,kin->jin", onehot, partial_sums, precision=lax.Precision.HIGHEST)
        total = lax.psum(summed, "sens")
        residual = (total - targets[t].reshape(blocks, block, samples)).astype(jnp.bfloat16)
        gradient = jnp.einsum(
            "kin,nkl->kil", jnp.take(residual, acts, axis=0), now, preferred_element_type=jnp.float32
        )
        weights = jnp.where(live[:, None, None], weights - step_rate * gradient, weights)
    return weights, residual.reshape(rows, samples)


def per_device(slopes, targets, reconstructor, foot_act, foot_slope, foot_count):
    block = reconstructor.shape[-1]
    slots = reconstructor.shape[2]
    groups = slopes.shape[2] // block
    samp_dev = slopes.shape[1]
    samples = targets.shape[2]
    devices = foot_slope.shape[1]
    step_rate = slots * block / (samples + 3 * slots * block)
    order = ORDERS.get(devices, tuple(range(devices)))
    packed = pack(order, foot_slope[0], slopes)
    arrived = lax.all_to_all(
        packed, "samp", split_axis=0, concat_axis=0, tiled=True, axis_index_groups=[list(order)]
    )
    weights = reconstructor[0, 0]
    if lax.axis_size("sens") > 1 or devices * STEPS * samp_dev != 2 * block or targets.shape[1] != 2 * block:
        own_index = lax.axis_index("samp")

        def own(table):
            return lax.dynamic_index_in_dim(table, own_index, 0, keepdims=False)

        places = own_places(own(foot_slope[0]), own(foot_count[0]), groups)
        fitted, residual = fit_over_groups(
            step_rate, samp_dev, order, places, own(foot_act[0]), arrived, weights, targets
        )
        return fitted[None, None], residual
    blocks = targets.shape[1] // block
    holder, kept = plan(groups, blocks, foot_slope[0], foot_act[0], foot_count, weights)
    seen = arrived.reshape(devices * STEPS * samp_dev, DISTINCT * block)
    fitted, residual = fit(step_rate, samp_dev, order, holder, seen, weights, targets, kept)
    return fitted[None, None], residual


def solution(mesh):
    return jax.shard_map(
        per_device,
        mesh=mesh,
        in_specs=(
            P(None, "samp", "sens"),
            P(None, "samp", None),
            P("sens", "samp", None, None, None),
            P("sens", None, None),
            P("sens", None, None),
            P("sens", None),
        ),
        out_specs=(P("sens", "samp", None, None, None), P("samp", None)),
        check_vma=False,
    )
```

```python
import functools

import jax
import jax.numpy as jnp
from jax import lax
from jax.experimental import pallas as pl
from jax.experimental.pallas import tpu as pltpu
from jax.sharding import PartitionSpec as P

STEPS = 2
DISTINCT = 20
BLOCK = 128
ORDERS = {
    32: (10, 22, 11, 9, 31, 25, 3, 5, 2, 14, 24, 13, 28, 27, 4, 12, 7, 15, 19, 16, 29, 20, 6, 21, 26, 1, 23, 8, 18, 17, 0, 30),
}
MIB = 1 << 20


def own_places(blocks_own, count_own, groups):
    ids = jnp.arange(blocks_own.shape[0])
    half = groups // 2
    turned = jnp.where(blocks_own >= groups - half, blocks_own - (groups - half), blocks_own + half)
    straight = blocks_own - jnp.min(blocks_own)
    around = turned - jnp.min(turned)
    same = blocks_own[:, None] == blocks_own[None, :]
    before = ids[None, :] < ids[:, None]
    first = ~jnp.any(same & before, axis=1)
    rank = jnp.sum(first[None, :] & before, axis=1)
    ranked = jnp.sum(jnp.where(same & first[None, :], rank[None, :], 0), axis=1)
    place = jnp.where(
        jnp.max(straight) < DISTINCT, straight, jnp.where(jnp.max(around) < DISTINCT, around, ranked)
    )
    return jnp.where(ids < count_own, place, -1).astype(jnp.int32)


def pack_kernel(
    pieces, order, blocks_hbm, slopes, out, blocks_of, rows, starts, turns, table, sems, load_sems, table_sems
):
    steps, samp_dev, width = slopes.shape
    groups = width // BLOCK
    devices, _, window = out.shape
    span = window // BLOCK
    slots = blocks_of.shape[1]
    half = groups // 2

    read_table = pltpu.make_async_copy(blocks_hbm, blocks_of, table_sems.at[0])
    read_table.start()
    parts = [(groups * i // pieces, groups * (i + 1) // pieces, 0) for i in range(pieces)] + [(0, span, groups)]
    loads = []
    for i, (first, last, shift) in enumerate(parts):
        for t in range(steps):
            source = slopes.at[t, :, pl.ds(first * BLOCK, (last - first) * BLOCK)]
            target = rows.at[pl.ds(t * samp_dev, samp_dev), pl.ds((first + shift) * BLOCK, (last - first) * BLOCK)]
            loads.append(pltpu.make_async_copy(source, target, load_sems.at[i, t]))
    for load in loads:
        load.start()

    read_table.wait()
    blocks = blocks_of[...].astype(jnp.float32)
    turned = jnp.where(blocks >= groups - half, blocks - (groups - half), blocks + half)

    def extent(named):
        low = jnp.min(named, axis=1, keepdims=True)
        return low, jnp.max(named, axis=1, keepdims=True) - low < DISTINCT

    low, fits = extent(blocks)
    low_turned, fits_turned = extent(turned)
    unturned = jnp.where(low_turned >= half, low_turned - half, low_turned + (groups - half))
    first = jnp.where(fits, low, jnp.where(fits_turned, unturned, -1.0)).astype(jnp.int32)
    first_of = [first[d, 0] for d in range(devices)]
    least = functools.reduce(jnp.minimum, first_of)
    for load in loads:
        load.wait()

    def to_turn(r, group, at, count):
        return pltpu.make_async_copy(
            rows.at[:, pl.ds(pl.multiple_of(group * BLOCK, BLOCK), count * BLOCK)],
            out.at[r, :, pl.ds(pl.multiple_of(at * BLOCK, BLOCK), count * BLOCK)],
            sems.at[r],
        )

    @pl.when(least >= 0)
    def _():
        for r, d in enumerate(order):
            to_turn(r, first_of[d], 0, span).start()

    @pl.when(least < 0)
    def _():
        for r, d in enumerate(order):
            starts[r] = first_of[d]
            turns[r] = jnp.int32(d)
        copy_table = pltpu.make_async_copy(blocks_of, table, table_sems.at[1])
        copy_table.start()
        copy_table.wait()

        def one_by_one(r):
            d = turns[r]

            def slot(k, placed):
                group = table[d, k]
                seen = lax.fori_loop(0, k, lambda j, s: jnp.where(table[d, j] == group, 1, s), jnp.int32(0))

                @pl.when(seen == 0)
                def _():
                    to_turn(r, group, placed, 1).start()

                return placed + 1 - seen

            placed = lax.fori_loop(0, slots, slot, jnp.int32(0))

            def fill(j, carry):
                to_turn(r, table[d, 0], j, 1).start()
                return carry

            lax.fori_loop(placed, span, fill, 0)

        def send(r, carry):
            @pl.when(starts[r] >= 0)
            def _():
                to_turn(r, starts[r], 0, span).start()

            @pl.when(starts[r] < 0)
            def _():
                one_by_one(r)

            return carry

        lax.fori_loop(0, devices, send, 0)

    for r in range(devices):
        to_turn(r, 0, 0, span).wait()


def pack(order, blocks_of, slopes, pieces=1):
    steps, samp_dev, width = slopes.shape
    devices, slots = blocks_of.shape
    tall = steps * samp_dev
    window = DISTINCT * BLOCK
    return pl.pallas_call(
        functools.partial(pack_kernel, pieces, order),
        out_shape=pltpu.HBM((devices, tall, window), slopes.dtype),
        in_specs=[pl.BlockSpec(memory_space=pltpu.HBM)] * 2,
        out_specs=pl.BlockSpec(memory_space=pltpu.HBM),
        scratch_shapes=[
            pltpu.VMEM((devices, slots), jnp.int32),
            pltpu.VMEM((tall, width + window), slopes.dtype),
            pltpu.SMEM((devices,), jnp.int32),
            pltpu.SMEM((devices,), jnp.int32),
            pltpu.SMEM((devices, slots), jnp.int32),
            pltpu.SemaphoreType.DMA((devices,)),
            pltpu.SemaphoreType.DMA((pieces + 1, steps)),
            pltpu.SemaphoreType.DMA((2,)),
        ],
        compiler_params=pltpu.CompilerParams(vmem_limit_bytes=16 * MIB),
        name="pack_windows",
    )(pltpu.with_memory_space_constraint(blocks_of, pltpu.HBM), pltpu.with_memory_space_constraint(slopes, pltpu.HBM))


def plan_kernel(
    groups, blocks, slope_tab, act_tab, count_tab, weights,
    holder_out, kept,
    slopes, acts, counts, places, holder, table_sems, kept_sems, holder_sem,
):
    slots = weights.shape[0]
    loads = [
        pltpu.make_async_copy(source, held, table_sems.at[i])
        for i, (source, held) in enumerate(((slope_tab, slopes), (act_tab, acts), (count_tab, counts)))
    ]
    for load in loads:
        load.start()
    for load in loads:
        load.wait()
    own = lax.axis_index("samp")
    count = counts[0, own]
    half = groups // 2

    def turn(group):
        return jnp.where(group >= groups - half, group - (groups - half), group + half)

    def extent(k, spans):
        low_end, high_end, low_turned, high_turned = spans
        group = slopes[own, k]
        turned = turn(group)
        return (
            jnp.minimum(low_end, group), jnp.maximum(high_end, group),
            jnp.minimum(low_turned, turned), jnp.maximum(high_turned, turned),
        )

    first = slopes[own, 0]
    low_end, high_end, low_turned, high_turned = lax.fori_loop(
        1, slots, extent, (first, first, turn(first), turn(first))
    )
    straight = high_end - low_end < DISTINCT
    around = high_turned - low_turned < DISTINCT

    def clear(j, carry):
        holder[0, j] = jnp.int32(-1)
        return carry

    lax.fori_loop(0, holder.shape[1], clear, 0)

    def rank(k, placed):
        group = slopes[own, k]
        found = lax.fori_loop(0, k, lambda j, at: jnp.where(slopes[own, j] == group, places[j], at), jnp.int32(-1))
        places[k] = jnp.where(found >= 0, found, placed)
        return jnp.where(found >= 0, placed, placed + 1)

    @pl.when(jnp.logical_not(jnp.logical_or(straight, around)))
    def _():
        lax.fori_loop(0, slots, rank, jnp.int32(0))

    @pl.when(jnp.logical_or(straight, around))
    def _():
        def offset(k, carry):
            group = slopes[own, k]
            places[k] = jnp.where(straight, group - low_end, turn(group) - low_turned)
            return carry

        lax.fori_loop(0, slots, offset, 0)

    def keep(k):
        return pltpu.make_async_copy(weights.at[k], kept.at[k], kept_sems.at[k])

    def start_keep(k, carry):
        keep(k).start()
        return carry

    def wait_keep(k, carry):
        keep(k).wait()
        return carry

    lax.fori_loop(count, slots, start_keep, 0)

    def lay(k, carry):
        holder[0, places[k] * blocks + acts[own, k]] = k
        return carry

    lax.fori_loop(0, count, lay, 0)
    store = pltpu.make_async_copy(holder, holder_out, holder_sem)
    store.start()
    store.wait()
    lax.fori_loop(count, slots, wait_keep, 0)


def plan(groups, blocks, slope_tab, act_tab, count_tab, weights):
    slots = weights.shape[0]
    vmem = pl.BlockSpec(memory_space=pltpu.VMEM)
    hbm = pl.BlockSpec(memory_space=pltpu.HBM)
    return pl.pallas_call(
        functools.partial(plan_kernel, groups, blocks),
        out_shape=[pltpu.VMEM((1, BLOCK), jnp.int32), pltpu.HBM(weights.shape, jnp.float32)],
        in_specs=[hbm, hbm, hbm, vmem],
        out_specs=[vmem, hbm],
        scratch_shapes=[
            pltpu.SMEM(slope_tab.shape, jnp.int32),
            pltpu.SMEM(act_tab.shape, jnp.int32),
            pltpu.SMEM(count_tab.shape, jnp.int32),
            pltpu.SMEM((slots,), jnp.int32),
            pltpu.SMEM((1, BLOCK), jnp.int32),
            pltpu.SemaphoreType.DMA((3,)),
            pltpu.SemaphoreType.DMA((slots,)),
            pltpu.SemaphoreType.DMA,
        ],
        compiler_params=pltpu.CompilerParams(vmem_limit_bytes=16 * MIB),
        cost_estimate=pl.CostEstimate(flops=10**6, bytes_accessed=4 * 10**6, transcendentals=0),
        name="plan_cells",
    )(
        pltpu.with_memory_space_constraint(slope_tab, pltpu.HBM),
        pltpu.with_memory_space_constraint(act_tab, pltpu.HBM),
        pltpu.with_memory_space_constraint(count_tab, pltpu.HBM),
        weights,
    )


def mixer(shape, samples, samp_dev, order, dtype):
    steps = shape[0] // samples
    tall = steps * samp_dev
    line = lax.broadcasted_iota(jnp.int32, (1, shape[1]), 1)
    turn, inner = line // tall, line % tall
    source = turn
    if order != tuple(range(len(order))):
        source = functools.reduce(jnp.add, [jnp.where(turn == r, d, 0) for r, d in enumerate(order)])
    row = (inner // samp_dev) * samples + source * samp_dev + inner % samp_dev
    return (lax.broadcasted_iota(jnp.int32, shape, 0) == row).astype(jnp.float32).astype(dtype), inner // samp_dev


def fit_kernel(
    step_rate, samp_dev, order, holder, seen, weights, targets, kept,
    fitted, residual, stack, rest_low, out_sems, rest_sem, *sums,
):
    steps, rows, samples = targets.shape
    count, block, _ = stack.shape
    wide, window = seen.shape
    blocks = rows // block
    pair = wide // block
    tiles = window // wide
    slot_of = [holder[0, j] for j in range(count)]

    def region(tile, part):
        return sums[part * 2 + tile % 2]

    def cell(tile, q, a):
        return (tile * pair + q) * blocks + a

    def held(j):
        return weights[jnp.maximum(slot_of[j], 0)]

    def live(j, value):
        return jnp.where(slot_of[j] >= 0, value, 0.0)

    def join(parts):
        return jnp.concatenate([jnp.concatenate(line, axis=1) for line in parts], axis=0)

    def multiply(tile, lhs, rhs, part, transpose=False):
        stage = (tile // 2) % 2
        pltpu.matmul_push_rhs(rhs, stage, tile % 2, transpose=transpose)
        pltpu.matmul_acc_lhs(region(tile, part), lhs, load_staged_rhs=stage)

    def tile_of(tile):
        return seen[:, tile * wide : (tile + 1) * wide]

    mix, step_of = mixer((steps * samples, wide), samples, samp_dev, order, jnp.bfloat16)
    multiply(0, jnp.concatenate([targets[t] for t in range(steps)], axis=1), mix, 1)
    for tile in range(tiles):
        cells = [[cell(tile, q, a) for q in range(pair)] for a in range(blocks)]
        start = join([[live(j, held(j)) for j in line] for line in cells]).astype(jnp.bfloat16)
        multiply(tile, start, tile_of(tile), 0, transpose=True)
    wanted = pltpu.matmul_pop(region(0, 1))
    store_rest = pltpu.make_async_copy(rest_low, residual, rest_sem)
    both = jnp.zeros((rows, wide), jnp.bfloat16)
    for t in range(steps):
        predicted = pltpu.matmul_pop(region(0, 0)) + pltpu.matmul_pop(region(1, 0))
        both = jnp.where(step_of == t, (predicted - wanted).astype(jnp.bfloat16), both)
        multiply(0, both, tile_of(0), 1)
        multiply(1, both, tile_of(1), 1)
        for tile in range(tiles):
            if t == steps - 1 and tile == 1:
                multiply(0, both, mix, 0, transpose=True)
            if t == steps - 1 and tile == 3:
                last = pltpu.matmul_pop(region(0, 0))
                rest_low[...] = last[:, t * samples : (t + 1) * samples].astype(rest_low.dtype)
                store_rest.start()
            gradient = pltpu.matmul_pop(region(tile, 1 + (tile // 2) % 2))
            if tile + 2 < tiles:
                multiply(tile + 2, both, tile_of(tile + 2), 1 + (tile // 2 + 1) % 2)
            parts = []
            for a in range(blocks):
                line = []
                for q in range(pair):
                    j = cell(tile, q, a)
                    moved = gradient[a * block : (a + 1) * block, q * block : (q + 1) * block]
                    new = held(j) - step_rate * moved
                    if t < steps - 1:
                        line.append(live(j, new))
                    else:
                        stack[j] = new
                parts.append(line)
            if t < steps - 1:
                multiply(tile, join(parts).astype(jnp.bfloat16), tile_of(tile), 0, transpose=True)
            else:
                for a in range(blocks):
                    for q in range(pair):
                        j = cell(tile, q, a)

                        @pl.when(slot_of[j] >= 0)
                        def _(j=j):
                            pltpu.make_async_copy(stack.at[j], fitted.at[slot_of[j]], out_sems.at[j]).start()

    store_rest.wait()
    for j in range(count):

        @pl.when(slot_of[j] >= 0)
        def _(j=j):
            pltpu.make_async_copy(stack.at[j], fitted.at[0], out_sems.at[j]).wait()


def fit(step_rate, samp_dev, order, holder, seen, weights, targets, kept):
    steps, rows, samples = targets.shape
    slots, block, _ = weights.shape
    wide, window = seen.shape
    count = rows // block * DISTINCT
    vmem = pl.BlockSpec(memory_space=pltpu.VMEM)
    hbm = pl.BlockSpec(memory_space=pltpu.HBM)

    def kernel(*refs):
        pl.run_scoped(
            functools.partial(fit_kernel, step_rate, samp_dev, order, *refs),
            *[pltpu.ACC(unit)((rows, wide), jnp.float32) for part in range(3) for unit in range(2)],
        )

    return pl.pallas_call(
        kernel,
        out_shape=[
            pltpu.HBM(kept.shape, jnp.float32),
            pltpu.HBM((rows, samples), jnp.bfloat16),
        ],
        in_specs=[vmem, vmem, vmem, vmem, hbm],
        out_specs=[hbm, hbm],
        input_output_aliases={4: 0},
        scratch_shapes=[
            pltpu.VMEM((count, block, block), jnp.float32),
            pltpu.VMEM((rows, samples), jnp.bfloat16),
            pltpu.SemaphoreType.DMA((count,)),
            pltpu.SemaphoreType.DMA,
        ],
        compiler_params=pltpu.CompilerParams(vmem_limit_bytes=24 * MIB),
        name="fit_steps",
    )(pltpu.with_memory_space_constraint(holder, pltpu.VMEM), seen, weights, targets, kept)


def fit_over_groups(step_rate, samp_dev, order, places, acts, arrived, weights, targets):
    steps, rows, samples = targets.shape
    slots, block, _ = weights.shape
    live = places >= 0
    devices = arrived.shape[0]
    if order != tuple(range(devices)):
        arrived = jnp.stack([arrived[order.index(d)] for d in range(devices)])
    grouped = arrived.reshape(devices, steps, samp_dev, DISTINCT, block)
    slot_slopes = jnp.take(grouped, jnp.maximum(places, 0), axis=3)
    blocks = rows // block
    onehot = ((acts[None, :] == jnp.arange(blocks)[:, None]) & live[None, :]).astype(jnp.float32)
    residual = None
    for t in range(steps):
        now = slot_slopes[:, t].reshape(samples, slots, block)
        partial_sums = jnp.einsum(
            "kil,nkl->kin", weights.astype(jnp.bfloat16), now, preferred_element_type=jnp.float32
        )
        summed = jnp.einsum("jk,kin->jin", onehot, partial_sums, precision=lax.Precision.HIGHEST)
        total = lax.psum(summed, "sens")
        residual = (total - targets[t].reshape(blocks, block, samples)).astype(jnp.bfloat16)
        gradient = jnp.einsum(
            "kin,nkl->kil", jnp.take(residual, acts, axis=0), now, preferred_element_type=jnp.float32
        )
        weights = jnp.where(live[:, None, None], weights - step_rate * gradient, weights)
    return weights, residual.reshape(rows, samples)


def per_device(slopes, targets, reconstructor, foot_act, foot_slope, foot_count):
    block = reconstructor.shape[-1]
    slots = reconstructor.shape[2]
    groups = slopes.shape[2] // block
    samp_dev = slopes.shape[1]
    samples = targets.shape[2]
    devices = foot_slope.shape[1]
    step_rate = slots * block / (samples + 3 * slots * block)
    order = ORDERS.get(devices, tuple(range(devices)))
    packed = pack(order, foot_slope[0], slopes)
    arrived = lax.all_to_all(
        packed, "samp", split_axis=0, concat_axis=0, tiled=True, axis_index_groups=[list(order)]
    )
    weights = reconstructor[0, 0]
    if lax.axis_size("sens") > 1 or devices * STEPS * samp_dev != 2 * block or targets.shape[1] != 2 * block:
        own_index = lax.axis_index("samp")

        def own(table):
            return lax.dynamic_index_in_dim(table, own_index, 0, keepdims=False)

        places = own_places(own(foot_slope[0]), own(foot_count[0]), groups)
        fitted, residual = fit_over_groups(
            step_rate, samp_dev, order, places, own(foot_act[0]), arrived, weights, targets
        )
        return fitted[None, None], residual
    blocks = targets.shape[1] // block
    holder, kept = plan(groups, blocks, foot_slope[0], foot_act[0], foot_count, weights)
    seen = arrived.reshape(devices * STEPS * samp_dev, DISTINCT * block)
    fitted, residual = fit(step_rate, samp_dev, order, holder, seen, weights, targets, kept)
    return fitted[None, None], residual


def solution(mesh):
    return jax.shard_map(
        per_device,
        mesh=mesh,
        in_specs=(
            P(None, "samp", "sens"),
            P(None, "samp", None),
            P("sens", "samp", None, None, None),
            P("sens", None, None),
            P("sens", None, None),
            P("sens", None),
        ),
        out_specs=(P("sens", "samp", None, None, None), P("samp", None)),
        check_vma=False,
    )
```

```python
import functools

import jax
import jax.numpy as jnp
from jax import lax
from jax.experimental import pallas as pl
from jax.experimental.pallas import tpu as pltpu
from jax.sharding import PartitionSpec as P

STEPS = 2
DISTINCT = 20
BLOCK = 128
ORDERS = {
    32: (10, 22, 11, 9, 31, 25, 3, 5, 2, 14, 24, 13, 28, 27, 4, 12, 7, 15, 19, 16, 29, 20, 6, 21, 26, 1, 23, 8, 18, 17, 0, 30),
}
MIB = 1 << 20


def own_places(blocks_own, count_own, groups):
    ids = jnp.arange(blocks_own.shape[0])
    half = groups // 2
    turned = jnp.where(blocks_own >= groups - half, blocks_own - (groups - half), blocks_own + half)
    straight = blocks_own - jnp.min(blocks_own)
    around = turned - jnp.min(turned)
    same = blocks_own[:, None] == blocks_own[None, :]
    before = ids[None, :] < ids[:, None]
    first = ~jnp.any(same & before, axis=1)
    rank = jnp.sum(first[None, :] & before, axis=1)
    ranked = jnp.sum(jnp.where(same & first[None, :], rank[None, :], 0), axis=1)
    place = jnp.where(
        jnp.max(straight) < DISTINCT, straight, jnp.where(jnp.max(around) < DISTINCT, around, ranked)
    )
    return jnp.where(ids < count_own, place, -1).astype(jnp.int32)


def pack_kernel(
    pieces, order, blocks_hbm, slopes, out, blocks_of, rows, starts, turns, table, sems, load_sems, table_sems
):
    steps, samp_dev, width = slopes.shape
    groups = width // BLOCK
    devices, _, window = out.shape
    span = window // BLOCK
    slots = blocks_of.shape[1]
    half = groups // 2

    read_table = pltpu.make_async_copy(blocks_hbm, blocks_of, table_sems.at[0])
    read_table.start()
    parts = [(groups * i // pieces, groups * (i + 1) // pieces, 0) for i in range(pieces)] + [(0, span, groups)]
    loads = []
    for i, (first, last, shift) in enumerate(parts):
        for t in range(steps):
            source = slopes.at[t, :, pl.ds(first * BLOCK, (last - first) * BLOCK)]
            target = rows.at[pl.ds(t * samp_dev, samp_dev), pl.ds((first + shift) * BLOCK, (last - first) * BLOCK)]
            loads.append(pltpu.make_async_copy(source, target, load_sems.at[i, t]))
    for load in loads:
        load.start()

    read_table.wait()
    blocks = blocks_of[...].astype(jnp.float32)
    turned = jnp.where(blocks >= groups - half, blocks - (groups - half), blocks + half)

    def extent(named):
        low = jnp.min(named, axis=1, keepdims=True)
        return low, jnp.max(named, axis=1, keepdims=True) - low < DISTINCT

    low, fits = extent(blocks)
    low_turned, fits_turned = extent(turned)
    unturned = jnp.where(low_turned >= half, low_turned - half, low_turned + (groups - half))
    first = jnp.where(fits, low, jnp.where(fits_turned, unturned, -1.0)).astype(jnp.int32)
    first_of = [first[d, 0] for d in range(devices)]
    least = functools.reduce(jnp.minimum, first_of)
    for load in loads:
        load.wait()

    def to_turn(r, group, at, count):
        return pltpu.make_async_copy(
            rows.at[:, pl.ds(pl.multiple_of(group * BLOCK, BLOCK), count * BLOCK)],
            out.at[r, :, pl.ds(pl.multiple_of(at * BLOCK, BLOCK), count * BLOCK)],
            sems.at[r],
        )

    @pl.when(least >= 0)
    def _():
        for r, d in enumerate(order):
            to_turn(r, first_of[d], 0, span).start()

    @pl.when(least < 0)
    def _():
        for r, d in enumerate(order):
            starts[r] = first_of[d]
            turns[r] = jnp.int32(d)
        copy_table = pltpu.make_async_copy(blocks_of, table, table_sems.at[1])
        copy_table.start()
        copy_table.wait()

        def one_by_one(r):
            d = turns[r]

            def slot(k, placed):
                group = table[d, k]
                seen = lax.fori_loop(0, k, lambda j, s: jnp.where(table[d, j] == group, 1, s), jnp.int32(0))

                @pl.when(seen == 0)
                def _():
                    to_turn(r, group, placed, 1).start()

                return placed + 1 - seen

            placed = lax.fori_loop(0, slots, slot, jnp.int32(0))

            def fill(j, carry):
                to_turn(r, table[d, 0], j, 1).start()
                return carry

            lax.fori_loop(placed, span, fill, 0)

        def send(r, carry):
            @pl.when(starts[r] >= 0)
            def _():
                to_turn(r, starts[r], 0, span).start()

            @pl.when(starts[r] < 0)
            def _():
                one_by_one(r)

            return carry

        lax.fori_loop(0, devices, send, 0)

    for r in range(devices):
        to_turn(r, 0, 0, span).wait()


def pack(order, blocks_of, slopes, pieces=1):
    steps, samp_dev, width = slopes.shape
    devices, slots = blocks_of.shape
    tall = steps * samp_dev
    window = DISTINCT * BLOCK
    return pl.pallas_call(
        functools.partial(pack_kernel, pieces, order),
        out_shape=pltpu.HBM((devices, tall, window), slopes.dtype),
        in_specs=[pl.BlockSpec(memory_space=pltpu.HBM)] * 2,
        out_specs=pl.BlockSpec(memory_space=pltpu.HBM),
        scratch_shapes=[
            pltpu.VMEM((devices, slots), jnp.int32),
            pltpu.VMEM((tall, width + window), slopes.dtype),
            pltpu.SMEM((devices,), jnp.int32),
            pltpu.SMEM((devices,), jnp.int32),
            pltpu.SMEM((devices, slots), jnp.int32),
            pltpu.SemaphoreType.DMA((devices,)),
            pltpu.SemaphoreType.DMA((pieces + 1, steps)),
            pltpu.SemaphoreType.DMA((2,)),
        ],
        compiler_params=pltpu.CompilerParams(vmem_limit_bytes=16 * MIB),
        name="pack_windows",
    )(pltpu.with_memory_space_constraint(blocks_of, pltpu.HBM), pltpu.with_memory_space_constraint(slopes, pltpu.HBM))


def plan_kernel(
    groups, blocks, slope_tab, act_tab, count_tab, weights_hbm,
    holder_out, kept, weights,
    slopes, acts, counts, places, holder, table_sems, kept_sems, holder_sem, weights_sem,
):
    slots = weights.shape[0]
    loads = [
        pltpu.make_async_copy(source, held, table_sems.at[i])
        for i, (source, held) in enumerate(((slope_tab, slopes), (act_tab, acts), (count_tab, counts)))
    ]
    for load in loads:
        load.start()
    load_weights = pltpu.make_async_copy(weights_hbm, weights, weights_sem)
    load_weights.start()
    for load in loads:
        load.wait()
    own = lax.axis_index("samp")
    count = counts[0, own]
    half = groups // 2

    def turn(group):
        return jnp.where(group >= groups - half, group - (groups - half), group + half)

    def extent(k, spans):
        low_end, high_end, low_turned, high_turned = spans
        group = slopes[own, k]
        turned = turn(group)
        return (
            jnp.minimum(low_end, group), jnp.maximum(high_end, group),
            jnp.minimum(low_turned, turned), jnp.maximum(high_turned, turned),
        )

    first = slopes[own, 0]
    low_end, high_end, low_turned, high_turned = lax.fori_loop(
        1, slots, extent, (first, first, turn(first), turn(first))
    )
    straight = high_end - low_end < DISTINCT
    around = high_turned - low_turned < DISTINCT

    def clear(j, carry):
        holder[0, j] = jnp.int32(-1)
        return carry

    lax.fori_loop(0, holder.shape[1], clear, 0)

    def rank(k, placed):
        group = slopes[own, k]
        found = lax.fori_loop(0, k, lambda j, at: jnp.where(slopes[own, j] == group, places[j], at), jnp.int32(-1))
        places[k] = jnp.where(found >= 0, found, placed)
        return jnp.where(found >= 0, placed, placed + 1)

    @pl.when(jnp.logical_not(jnp.logical_or(straight, around)))
    def _():
        lax.fori_loop(0, slots, rank, jnp.int32(0))

    @pl.when(jnp.logical_or(straight, around))
    def _():
        def offset(k, carry):
            group = slopes[own, k]
            places[k] = jnp.where(straight, group - low_end, turn(group) - low_turned)
            return carry

        lax.fori_loop(0, slots, offset, 0)

    def keep(k):
        return pltpu.make_async_copy(weights.at[k], kept.at[k], kept_sems.at[k])

    def start_keep(k, carry):
        keep(k).start()
        return carry

    def wait_keep(k, carry):
        keep(k).wait()
        return carry

    load_weights.wait()
    lax.fori_loop(count, slots, start_keep, 0)

    def lay(k, carry):
        holder[0, places[k] * blocks + acts[own, k]] = k
        return carry

    lax.fori_loop(0, count, lay, 0)
    store = pltpu.make_async_copy(holder, holder_out, holder_sem)
    store.start()
    store.wait()
    lax.fori_loop(count, slots, wait_keep, 0)


def plan(groups, blocks, slope_tab, act_tab, count_tab, weights):
    slots = weights.shape[0]
    vmem = pl.BlockSpec(memory_space=pltpu.VMEM)
    hbm = pl.BlockSpec(memory_space=pltpu.HBM)
    return pl.pallas_call(
        functools.partial(plan_kernel, groups, blocks),
        out_shape=[
            pltpu.VMEM((1, BLOCK), jnp.int32),
            pltpu.HBM(weights.shape, jnp.float32),
            pltpu.VMEM(weights.shape, jnp.float32),
        ],
        in_specs=[hbm, hbm, hbm, hbm],
        out_specs=[vmem, hbm, vmem],
        scratch_shapes=[
            pltpu.SMEM(slope_tab.shape, jnp.int32),
            pltpu.SMEM(act_tab.shape, jnp.int32),
            pltpu.SMEM(count_tab.shape, jnp.int32),
            pltpu.SMEM((slots,), jnp.int32),
            pltpu.SMEM((1, BLOCK), jnp.int32),
            pltpu.SemaphoreType.DMA((3,)),
            pltpu.SemaphoreType.DMA((slots,)),
            pltpu.SemaphoreType.DMA,
            pltpu.SemaphoreType.DMA,
        ],
        compiler_params=pltpu.CompilerParams(vmem_limit_bytes=16 * MIB),
        cost_estimate=pl.CostEstimate(flops=10**6, bytes_accessed=4 * 10**6, transcendentals=0),
        name="plan_cells",
    )(
        pltpu.with_memory_space_constraint(slope_tab, pltpu.HBM),
        pltpu.with_memory_space_constraint(act_tab, pltpu.HBM),
        pltpu.with_memory_space_constraint(count_tab, pltpu.HBM),
        pltpu.with_memory_space_constraint(weights, pltpu.HBM),
    )


def mixer(shape, samples, samp_dev, order, dtype):
    steps = shape[0] // samples
    tall = steps * samp_dev
    line = lax.broadcasted_iota(jnp.int32, (1, shape[1]), 1)
    turn, inner = line // tall, line % tall
    source = turn
    if order != tuple(range(len(order))):
        source = functools.reduce(jnp.add, [jnp.where(turn == r, d, 0) for r, d in enumerate(order)])
    row = (inner // samp_dev) * samples + source * samp_dev + inner % samp_dev
    return (lax.broadcasted_iota(jnp.int32, shape, 0) == row).astype(jnp.float32).astype(dtype), inner // samp_dev


def fit_kernel(
    step_rate, samp_dev, order, holder, seen, weights, targets, kept,
    fitted, residual, stack, rest_low, out_sems, rest_sem, *sums,
):
    steps, rows, samples = targets.shape
    count, block, _ = stack.shape
    wide, window = seen.shape
    blocks = rows // block
    pair = wide // block
    tiles = window // wide
    slot_of = [holder[0, j] for j in range(count)]

    def region(tile, part):
        return sums[part * 2 + tile % 2]

    def cell(tile, q, a):
        return (tile * pair + q) * blocks + a

    def held(j):
        return weights[jnp.maximum(slot_of[j], 0)]

    def live(j, value):
        return jnp.where(slot_of[j] >= 0, value, 0.0)

    def join(parts):
        return jnp.concatenate([jnp.concatenate(line, axis=1) for line in parts], axis=0)

    def multiply(tile, lhs, rhs, part, transpose=False):
        stage = (tile // 2) % 2
        pltpu.matmul_push_rhs(rhs, stage, tile % 2, transpose=transpose)
        pltpu.matmul_acc_lhs(region(tile, part), lhs, load_staged_rhs=stage)

    def tile_of(tile):
        return seen[:, tile * wide : (tile + 1) * wide]

    mix, step_of = mixer((steps * samples, wide), samples, samp_dev, order, jnp.bfloat16)
    multiply(0, jnp.concatenate([targets[t] for t in range(steps)], axis=1), mix, 1)
    for tile in range(tiles):
        cells = [[cell(tile, q, a) for q in range(pair)] for a in range(blocks)]
        start = join([[live(j, held(j)) for j in line] for line in cells]).astype(jnp.bfloat16)
        multiply(tile, start, tile_of(tile), 0, transpose=True)
    wanted = pltpu.matmul_pop(region(0, 1))
    store_rest = pltpu.make_async_copy(rest_low, residual, rest_sem)
    both = jnp.zeros((rows, wide), jnp.bfloat16)
    for t in range(steps):
        predicted = pltpu.matmul_pop(region(0, 0)) + pltpu.matmul_pop(region(1, 0))
        both = jnp.where(step_of == t, (predicted - wanted).astype(jnp.bfloat16), both)
        multiply(0, both, tile_of(0), 1)
        multiply(1, both, tile_of(1), 1)
        for tile in range(tiles):
            if t == steps - 1 and tile == 1:
                multiply(0, both, mix, 0, transpose=True)
            if t == steps - 1 and tile == 3:
                last = pltpu.matmul_pop(region(0, 0))
                rest_low[...] = last[:, t * samples : (t + 1) * samples].astype(rest_low.dtype)
                store_rest.start()
            gradient = pltpu.matmul_pop(region(tile, 1 + (tile // 2) % 2))
            if tile + 2 < tiles:
                multiply(tile + 2, both, tile_of(tile + 2), 1 + (tile // 2 + 1) % 2)
            parts = []
            for a in range(blocks):
                line = []
                for q in range(pair):
                    j = cell(tile, q, a)
                    moved = gradient[a * block : (a + 1) * block, q * block : (q + 1) * block]
                    new = held(j) - step_rate * moved
                    if t < steps - 1:
                        line.append(live(j, new))
                    else:
                        stack[j] = new
                parts.append(line)
            if t < steps - 1:
                multiply(tile, join(parts).astype(jnp.bfloat16), tile_of(tile), 0, transpose=True)
            else:
                for a in range(blocks):
                    for q in range(pair):
                        j = cell(tile, q, a)

                        @pl.when(slot_of[j] >= 0)
                        def _(j=j):
                            pltpu.make_async_copy(stack.at[j], fitted.at[slot_of[j]], out_sems.at[j]).start()

    store_rest.wait()
    for j in range(count):

        @pl.when(slot_of[j] >= 0)
        def _(j=j):
            pltpu.make_async_copy(stack.at[j], fitted.at[0], out_sems.at[j]).wait()


def fit(step_rate, samp_dev, order, holder, seen, weights, targets, kept):
    steps, rows, samples = targets.shape
    slots, block, _ = weights.shape
    wide, window = seen.shape
    count = rows // block * DISTINCT
    vmem = pl.BlockSpec(memory_space=pltpu.VMEM)
    hbm = pl.BlockSpec(memory_space=pltpu.HBM)

    def kernel(*refs):
        pl.run_scoped(
            functools.partial(fit_kernel, step_rate, samp_dev, order, *refs),
            *[pltpu.ACC(unit)((rows, wide), jnp.float32) for part in range(3) for unit in range(2)],
        )

    return pl.pallas_call(
        kernel,
        out_shape=[
            pltpu.HBM(kept.shape, jnp.float32),
            pltpu.HBM((rows, samples), jnp.bfloat16),
        ],
        in_specs=[vmem, vmem, vmem, vmem, hbm],
        out_specs=[hbm, hbm],
        input_output_aliases={4: 0},
        scratch_shapes=[
            pltpu.VMEM((count, block, block), jnp.float32),
            pltpu.VMEM((rows, samples), jnp.bfloat16),
            pltpu.SemaphoreType.DMA((count,)),
            pltpu.SemaphoreType.DMA,
        ],
        compiler_params=pltpu.CompilerParams(vmem_limit_bytes=24 * MIB),
        name="fit_steps",
    )(
        pltpu.with_memory_space_constraint(holder, pltpu.VMEM),
        seen,
        pltpu.with_memory_space_constraint(weights, pltpu.VMEM),
        targets,
        kept,
    )


def fit_over_groups(step_rate, samp_dev, order, places, acts, arrived, weights, targets):
    steps, rows, samples = targets.shape
    slots, block, _ = weights.shape
    live = places >= 0
    devices = arrived.shape[0]
    if order != tuple(range(devices)):
        arrived = jnp.stack([arrived[order.index(d)] for d in range(devices)])
    grouped = arrived.reshape(devices, steps, samp_dev, DISTINCT, block)
    slot_slopes = jnp.take(grouped, jnp.maximum(places, 0), axis=3)
    blocks = rows // block
    onehot = ((acts[None, :] == jnp.arange(blocks)[:, None]) & live[None, :]).astype(jnp.float32)
    residual = None
    for t in range(steps):
        now = slot_slopes[:, t].reshape(samples, slots, block)
        partial_sums = jnp.einsum(
            "kil,nkl->kin", weights.astype(jnp.bfloat16), now, preferred_element_type=jnp.float32
        )
        summed = jnp.einsum("jk,kin->jin", onehot, partial_sums, precision=lax.Precision.HIGHEST)
        total = lax.psum(summed, "sens")
        residual = (total - targets[t].reshape(blocks, block, samples)).astype(jnp.bfloat16)
        gradient = jnp.einsum(
            "kin,nkl->kil", jnp.take(residual, acts, axis=0), now, preferred_element_type=jnp.float32
        )
        weights = jnp.where(live[:, None, None], weights - step_rate * gradient, weights)
    return weights, residual.reshape(rows, samples)


def per_device(slopes, targets, reconstructor, foot_act, foot_slope, foot_count):
    block = reconstructor.shape[-1]
    slots = reconstructor.shape[2]
    groups = slopes.shape[2] // block
    samp_dev = slopes.shape[1]
    samples = targets.shape[2]
    devices = foot_slope.shape[1]
    step_rate = slots * block / (samples + 3 * slots * block)
    order = ORDERS.get(devices, tuple(range(devices)))
    packed = pack(order, foot_slope[0], slopes)
    arrived = lax.all_to_all(
        packed, "samp", split_axis=0, concat_axis=0, tiled=True, axis_index_groups=[list(order)]
    )
    weights = reconstructor[0, 0]
    if lax.axis_size("sens") > 1 or devices * STEPS * samp_dev != 2 * block or targets.shape[1] != 2 * block:
        own_index = lax.axis_index("samp")

        def own(table):
            return lax.dynamic_index_in_dim(table, own_index, 0, keepdims=False)

        places = own_places(own(foot_slope[0]), own(foot_count[0]), groups)
        fitted, residual = fit_over_groups(
            step_rate, samp_dev, order, places, own(foot_act[0]), arrived, weights, targets
        )
        return fitted[None, None], residual
    blocks = targets.shape[1] // block
    holder, kept, weights = plan(groups, blocks, foot_slope[0], foot_act[0], foot_count, weights)
    seen = arrived.reshape(devices * STEPS * samp_dev, DISTINCT * block)
    fitted, residual = fit(step_rate, samp_dev, order, holder, seen, weights, targets, kept)
    return fitted[None, None], residual


def solution(mesh):
    return jax.shard_map(
        per_device,
        mesh=mesh,
        in_specs=(
            P(None, "samp", "sens"),
            P(None, "samp", None),
            P("sens", "samp", None, None, None),
            P("sens", None, None),
            P("sens", None, None),
            P("sens", None),
        ),
        out_specs=(P("sens", "samp", None, None, None), P("samp", None)),
        check_vma=False,
    )
```

```python
import functools

import jax
import jax.numpy as jnp
from jax import lax
from jax.experimental import pallas as pl
from jax.experimental.pallas import tpu as pltpu
from jax.sharding import PartitionSpec as P

STEPS = 2
DISTINCT = 20
BLOCK = 128
ORDERS = {
    32: (10, 22, 11, 9, 31, 25, 3, 5, 2, 14, 24, 13, 28, 27, 4, 12, 7, 15, 19, 16, 29, 20, 6, 21, 26, 1, 23, 8, 18, 17, 0, 30),
}
MIB = 1 << 20


def own_places(blocks_own, count_own, groups):
    ids = jnp.arange(blocks_own.shape[0])
    half = groups // 2
    turned = jnp.where(blocks_own >= groups - half, blocks_own - (groups - half), blocks_own + half)
    straight = blocks_own - jnp.min(blocks_own)
    around = turned - jnp.min(turned)
    same = blocks_own[:, None] == blocks_own[None, :]
    before = ids[None, :] < ids[:, None]
    first = ~jnp.any(same & before, axis=1)
    rank = jnp.sum(first[None, :] & before, axis=1)
    ranked = jnp.sum(jnp.where(same & first[None, :], rank[None, :], 0), axis=1)
    place = jnp.where(
        jnp.max(straight) < DISTINCT, straight, jnp.where(jnp.max(around) < DISTINCT, around, ranked)
    )
    return jnp.where(ids < count_own, place, -1).astype(jnp.int32)


def pack_kernel(
    pieces, order, blocks_hbm, slopes, out, blocks_of, rows, starts, turns, table, sems, load_sems, table_sems
):
    steps, samp_dev, width = slopes.shape
    groups = width // BLOCK
    devices, _, window = out.shape
    span = window // BLOCK
    slots = blocks_of.shape[1]
    half = groups // 2

    read_table = pltpu.make_async_copy(blocks_hbm, blocks_of, table_sems.at[0])
    read_table.start()
    parts = [(groups * i // pieces, groups * (i + 1) // pieces, 0) for i in range(pieces)] + [(0, span, groups)]
    loads = []
    for i, (first, last, shift) in enumerate(parts):
        for t in range(steps):
            source = slopes.at[t, :, pl.ds(first * BLOCK, (last - first) * BLOCK)]
            target = rows.at[pl.ds(t * samp_dev, samp_dev), pl.ds((first + shift) * BLOCK, (last - first) * BLOCK)]
            loads.append(pltpu.make_async_copy(source, target, load_sems.at[i, t]))
    for load in loads:
        load.start()

    read_table.wait()
    blocks = blocks_of[...].astype(jnp.float32)
    turned = jnp.where(blocks >= groups - half, blocks - (groups - half), blocks + half)

    def extent(named):
        low = jnp.min(named, axis=1, keepdims=True)
        return low, jnp.max(named, axis=1, keepdims=True) - low < DISTINCT

    low, fits = extent(blocks)
    low_turned, fits_turned = extent(turned)
    unturned = jnp.where(low_turned >= half, low_turned - half, low_turned + (groups - half))
    first = jnp.where(fits, low, jnp.where(fits_turned, unturned, -1.0)).astype(jnp.int32)
    first_of = [first[d, 0] for d in range(devices)]
    least = functools.reduce(jnp.minimum, first_of)
    for load in loads:
        load.wait()

    def to_turn(r, group, at, count):
        return pltpu.make_async_copy(
            rows.at[:, pl.ds(pl.multiple_of(group * BLOCK, BLOCK), count * BLOCK)],
            out.at[r, :, pl.ds(pl.multiple_of(at * BLOCK, BLOCK), count * BLOCK)],
            sems.at[r],
        )

    @pl.when(least >= 0)
    def _():
        for r, d in enumerate(order):
            to_turn(r, first_of[d], 0, span).start()

    @pl.when(least < 0)
    def _():
        for r, d in enumerate(order):
            starts[r] = first_of[d]
            turns[r] = jnp.int32(d)
        copy_table = pltpu.make_async_copy(blocks_of, table, table_sems.at[1])
        copy_table.start()
        copy_table.wait()

        def one_by_one(r):
            d = turns[r]

            def slot(k, placed):
                group = table[d, k]
                seen = lax.fori_loop(0, k, lambda j, s: jnp.where(table[d, j] == group, 1, s), jnp.int32(0))

                @pl.when(seen == 0)
                def _():
                    to_turn(r, group, placed, 1).start()

                return placed + 1 - seen

            placed = lax.fori_loop(0, slots, slot, jnp.int32(0))

            def fill(j, carry):
                to_turn(r, table[d, 0], j, 1).start()
                return carry

            lax.fori_loop(placed, span, fill, 0)

        def send(r, carry):
            @pl.when(starts[r] >= 0)
            def _():
                to_turn(r, starts[r], 0, span).start()

            @pl.when(starts[r] < 0)
            def _():
                one_by_one(r)

            return carry

        lax.fori_loop(0, devices, send, 0)

    for r in range(devices):
        to_turn(r, 0, 0, span).wait()


def pack(order, blocks_of, slopes, pieces=1):
    steps, samp_dev, width = slopes.shape
    devices, slots = blocks_of.shape
    tall = steps * samp_dev
    window = DISTINCT * BLOCK
    return pl.pallas_call(
        functools.partial(pack_kernel, pieces, order),
        out_shape=pltpu.HBM((devices, tall, window), slopes.dtype),
        in_specs=[pl.BlockSpec(memory_space=pltpu.HBM)] * 2,
        out_specs=pl.BlockSpec(memory_space=pltpu.HBM),
        scratch_shapes=[
            pltpu.VMEM((devices, slots), jnp.int32),
            pltpu.VMEM((tall, width + window), slopes.dtype),
            pltpu.SMEM((devices,), jnp.int32),
            pltpu.SMEM((devices,), jnp.int32),
            pltpu.SMEM((devices, slots), jnp.int32),
            pltpu.SemaphoreType.DMA((devices,)),
            pltpu.SemaphoreType.DMA((pieces + 1, steps)),
            pltpu.SemaphoreType.DMA((2,)),
        ],
        compiler_params=pltpu.CompilerParams(vmem_limit_bytes=16 * MIB),
        name="pack_windows",
    )(pltpu.with_memory_space_constraint(blocks_of, pltpu.HBM), pltpu.with_memory_space_constraint(slopes, pltpu.HBM))


def plan_kernel(
    groups, blocks, slope_tab, act_tab, count_tab, weights_hbm,
    holder_out, kept, weights,
    slopes, acts, counts, places, holder, table_sems, kept_sems, holder_sem, weights_sem,
):
    slots = weights.shape[0]
    loads = [
        pltpu.make_async_copy(source, held, table_sems.at[i])
        for i, (source, held) in enumerate(((slope_tab, slopes), (act_tab, acts), (count_tab, counts)))
    ]
    for load in loads:
        load.start()
    load_weights = pltpu.make_async_copy(weights_hbm, weights, weights_sem)
    load_weights.start()
    for load in loads:
        load.wait()
    own = lax.axis_index("samp")
    count = counts[0, own]
    half = groups // 2

    def turn(group):
        return jnp.where(group >= groups - half, group - (groups - half), group + half)

    def extent(k, spans):
        low_end, high_end, low_turned, high_turned = spans
        group = slopes[own, k]
        turned = turn(group)
        return (
            jnp.minimum(low_end, group), jnp.maximum(high_end, group),
            jnp.minimum(low_turned, turned), jnp.maximum(high_turned, turned),
        )

    first = slopes[own, 0]
    low_end, high_end, low_turned, high_turned = lax.fori_loop(
        1, slots, extent, (first, first, turn(first), turn(first))
    )
    straight = high_end - low_end < DISTINCT
    around = high_turned - low_turned < DISTINCT

    def clear(j, carry):
        holder[0, j] = jnp.int32(-1)
        return carry

    lax.fori_loop(0, holder.shape[1], clear, 0)

    def rank(k, placed):
        group = slopes[own, k]
        found = lax.fori_loop(0, k, lambda j, at: jnp.where(slopes[own, j] == group, places[j], at), jnp.int32(-1))
        places[k] = jnp.where(found >= 0, found, placed)
        return jnp.where(found >= 0, placed, placed + 1)

    @pl.when(jnp.logical_not(jnp.logical_or(straight, around)))
    def _():
        lax.fori_loop(0, slots, rank, jnp.int32(0))

    @pl.when(jnp.logical_or(straight, around))
    def _():
        def offset(k, carry):
            group = slopes[own, k]
            places[k] = jnp.where(straight, group - low_end, turn(group) - low_turned)
            return carry

        lax.fori_loop(0, slots, offset, 0)

    def keep(k):
        return pltpu.make_async_copy(weights.at[k], kept.at[k], kept_sems.at[k])

    def start_keep(k, carry):
        keep(k).start()
        return carry

    def wait_keep(k, carry):
        keep(k).wait()
        return carry

    load_weights.wait()
    lax.fori_loop(count, slots, start_keep, 0)

    def lay(k, carry):
        holder[0, places[k] * blocks + acts[own, k]] = k
        return carry

    lax.fori_loop(0, count, lay, 0)
    store = pltpu.make_async_copy(holder, holder_out, holder_sem)
    store.start()
    store.wait()
    lax.fori_loop(count, slots, wait_keep, 0)


def plan(groups, blocks, slope_tab, act_tab, count_tab, weights):
    slots = weights.shape[0]
    vmem = pl.BlockSpec(memory_space=pltpu.VMEM)
    hbm = pl.BlockSpec(memory_space=pltpu.HBM)
    return pl.pallas_call(
        functools.partial(plan_kernel, groups, blocks),
        out_shape=[
            pltpu.VMEM((1, BLOCK), jnp.int32),
            pltpu.HBM(weights.shape, jnp.float32),
            pltpu.VMEM(weights.shape, jnp.float32),
        ],
        in_specs=[hbm, hbm, hbm, hbm],
        out_specs=[vmem, hbm, vmem],
        scratch_shapes=[
            pltpu.SMEM(slope_tab.shape, jnp.int32),
            pltpu.SMEM(act_tab.shape, jnp.int32),
            pltpu.SMEM(count_tab.shape, jnp.int32),
            pltpu.SMEM((slots,), jnp.int32),
            pltpu.SMEM((1, BLOCK), jnp.int32),
            pltpu.SemaphoreType.DMA((3,)),
            pltpu.SemaphoreType.DMA((slots,)),
            pltpu.SemaphoreType.DMA,
            pltpu.SemaphoreType.DMA,
        ],
        compiler_params=pltpu.CompilerParams(vmem_limit_bytes=16 * MIB),
        cost_estimate=pl.CostEstimate(flops=10**6, bytes_accessed=4 * 10**6, transcendentals=0),
        name="plan_cells",
    )(
        pltpu.with_memory_space_constraint(slope_tab, pltpu.HBM),
        pltpu.with_memory_space_constraint(act_tab, pltpu.HBM),
        pltpu.with_memory_space_constraint(count_tab, pltpu.HBM),
        pltpu.with_memory_space_constraint(weights, pltpu.HBM),
    )


def mixer(shape, samples, samp_dev, order, dtype):
    steps = shape[0] // samples
    tall = steps * samp_dev
    line = lax.broadcasted_iota(jnp.int32, (1, shape[1]), 1)
    turn, inner = line // tall, line % tall
    source = turn
    if order != tuple(range(len(order))):
        source = functools.reduce(jnp.add, [jnp.where(turn == r, d, 0) for r, d in enumerate(order)])
    row = (inner // samp_dev) * samples + source * samp_dev + inner % samp_dev
    return (lax.broadcasted_iota(jnp.int32, shape, 0) == row).astype(jnp.float32).astype(dtype), inner // samp_dev


def fit_kernel(
    step_rate, samp_dev, order, holder, seen, weights, targets, kept,
    fitted, residual, stack, rest_low, out_sems, rest_sem, *sums,
):
    steps, rows, samples = targets.shape
    count, block, _ = stack.shape
    wide, window = seen.shape
    blocks = rows // block
    pair = wide // block
    tiles = window // wide
    slot_of = [holder[0, j] for j in range(count)]

    def region(tile, part):
        return sums[part * 2 + tile % 2]

    def cell(tile, q, a):
        return (tile * pair + q) * blocks + a

    def held(j):
        return weights[jnp.maximum(slot_of[j], 0)]

    def live(j, value):
        return jnp.where(slot_of[j] >= 0, value, 0.0)

    def join(parts):
        return jnp.concatenate([jnp.concatenate(line, axis=1) for line in parts], axis=0)

    def multiply(tile, lhs, rhs, part, transpose=False):
        stage = (tile // 2) % 2
        pltpu.matmul_push_rhs(rhs, stage, tile % 2, transpose=transpose)
        pltpu.matmul_acc_lhs(region(tile, part), lhs, load_staged_rhs=stage)

    def tile_of(tile):
        return seen[:, tile * wide : (tile + 1) * wide]

    mix, step_of = mixer((steps * samples, wide), samples, samp_dev, order, jnp.bfloat16)
    multiply(0, jnp.concatenate([targets[t] for t in range(steps)], axis=1), mix, 1)
    for tile in range(tiles):
        cells = [[cell(tile, q, a) for q in range(pair)] for a in range(blocks)]
        start = join([[live(j, held(j)) for j in line] for line in cells]).astype(jnp.bfloat16)
        multiply(tile, start, tile_of(tile), 0, transpose=True)
    wanted = pltpu.matmul_pop(region(0, 1))
    store_rest = pltpu.make_async_copy(rest_low, residual, rest_sem)
    both = jnp.zeros((rows, wide), jnp.bfloat16)
    for t in range(steps):
        predicted = pltpu.matmul_pop(region(0, 0)) + pltpu.matmul_pop(region(1, 0))
        both = jnp.where(step_of == t, (predicted - wanted).astype(jnp.bfloat16), both)
        multiply(0, both, tile_of(0), 1)
        multiply(1, both, tile_of(1), 1)
        for tile in range(tiles):
            if t == steps - 1 and tile == 1:
                multiply(0, both, mix, 0, transpose=True)
            if t == steps - 1 and tile == 3:
                last = pltpu.matmul_pop(region(0, 0))
                rest_low[...] = last[:, t * samples : (t + 1) * samples].astype(rest_low.dtype)
                store_rest.start()
            gradient = pltpu.matmul_pop(region(tile, 1 + (tile // 2) % 2))
            if tile + 2 < tiles:
                multiply(tile + 2, both, tile_of(tile + 2), 1 + (tile // 2 + 1) % 2)
            parts = []
            for a in range(blocks):
                line = []
                for q in range(pair):
                    j = cell(tile, q, a)
                    moved = gradient[a * block : (a + 1) * block, q * block : (q + 1) * block]
                    new = held(j) - step_rate * moved
                    if t < steps - 1:
                        line.append(live(j, new))
                    else:
                        stack[j] = new
                parts.append(line)
            if t < steps - 1:
                multiply(tile, join(parts).astype(jnp.bfloat16), tile_of(tile), 0, transpose=True)
            elif tile % 2 == 1 or tile == tiles - 1:
                for p in range(tile - tile % 2, tile + 1):
                    for j in range(cell(p, 0, 0), cell(p + 1, 0, 0)):

                        @pl.when(slot_of[j] >= 0)
                        def _(j=j):
                            pltpu.make_async_copy(stack.at[j], fitted.at[slot_of[j]], out_sems.at[j]).start()

    store_rest.wait()
    for j in range(count):

        @pl.when(slot_of[j] >= 0)
        def _(j=j):
            pltpu.make_async_copy(stack.at[j], fitted.at[0], out_sems.at[j]).wait()


def fit(step_rate, samp_dev, order, holder, seen, weights, targets, kept):
    steps, rows, samples = targets.shape
    slots, block, _ = weights.shape
    wide, window = seen.shape
    count = rows // block * DISTINCT
    vmem = pl.BlockSpec(memory_space=pltpu.VMEM)
    hbm = pl.BlockSpec(memory_space=pltpu.HBM)

    def kernel(*refs):
        pl.run_scoped(
            functools.partial(fit_kernel, step_rate, samp_dev, order, *refs),
            *[pltpu.ACC(unit)((rows, wide), jnp.float32) for part in range(3) for unit in range(2)],
        )

    return pl.pallas_call(
        kernel,
        out_shape=[
            pltpu.HBM(kept.shape, jnp.float32),
            pltpu.HBM((rows, samples), jnp.bfloat16),
        ],
        in_specs=[vmem, vmem, vmem, vmem, hbm],
        out_specs=[hbm, hbm],
        input_output_aliases={4: 0},
        scratch_shapes=[
            pltpu.VMEM((count, block, block), jnp.float32),
            pltpu.VMEM((rows, samples), jnp.bfloat16),
            pltpu.SemaphoreType.DMA((count,)),
            pltpu.SemaphoreType.DMA,
        ],
        compiler_params=pltpu.CompilerParams(vmem_limit_bytes=24 * MIB),
        name="fit_steps",
    )(
        pltpu.with_memory_space_constraint(holder, pltpu.VMEM),
        seen,
        pltpu.with_memory_space_constraint(weights, pltpu.VMEM),
        targets,
        kept,
    )


def fit_over_groups(step_rate, samp_dev, order, places, acts, arrived, weights, targets):
    steps, rows, samples = targets.shape
    slots, block, _ = weights.shape
    live = places >= 0
    devices = arrived.shape[0]
    if order != tuple(range(devices)):
        arrived = jnp.stack([arrived[order.index(d)] for d in range(devices)])
    grouped = arrived.reshape(devices, steps, samp_dev, DISTINCT, block)
    slot_slopes = jnp.take(grouped, jnp.maximum(places, 0), axis=3)
    blocks = rows // block
    onehot = ((acts[None, :] == jnp.arange(blocks)[:, None]) & live[None, :]).astype(jnp.float32)
    residual = None
    for t in range(steps):
        now = slot_slopes[:, t].reshape(samples, slots, block)
        partial_sums = jnp.einsum(
            "kil,nkl->kin", weights.astype(jnp.bfloat16), now, preferred_element_type=jnp.float32
        )
        summed = jnp.einsum("jk,kin->jin", onehot, partial_sums, precision=lax.Precision.HIGHEST)
        total = lax.psum(summed, "sens")
        residual = (total - targets[t].reshape(blocks, block, samples)).astype(jnp.bfloat16)
        gradient = jnp.einsum(
            "kin,nkl->kil", jnp.take(residual, acts, axis=0), now, preferred_element_type=jnp.float32
        )
        weights = jnp.where(live[:, None, None], weights - step_rate * gradient, weights)
    return weights, residual.reshape(rows, samples)


def per_device(slopes, targets, reconstructor, foot_act, foot_slope, foot_count):
    block = reconstructor.shape[-1]
    slots = reconstructor.shape[2]
    groups = slopes.shape[2] // block
    samp_dev = slopes.shape[1]
    samples = targets.shape[2]
    devices = foot_slope.shape[1]
    step_rate = slots * block / (samples + 3 * slots * block)
    order = ORDERS.get(devices, tuple(range(devices)))
    packed = pack(order, foot_slope[0], slopes)
    arrived = lax.all_to_all(
        packed, "samp", split_axis=0, concat_axis=0, tiled=True, axis_index_groups=[list(order)]
    )
    weights = reconstructor[0, 0]
    if lax.axis_size("sens") > 1 or devices * STEPS * samp_dev != 2 * block or targets.shape[1] != 2 * block:
        own_index = lax.axis_index("samp")

        def own(table):
            return lax.dynamic_index_in_dim(table, own_index, 0, keepdims=False)

        places = own_places(own(foot_slope[0]), own(foot_count[0]), groups)
        fitted, residual = fit_over_groups(
            step_rate, samp_dev, order, places, own(foot_act[0]), arrived, weights, targets
        )
        return fitted[None, None], residual
    blocks = targets.shape[1] // block
    holder, kept, weights = plan(groups, blocks, foot_slope[0], foot_act[0], foot_count, weights)
    seen = arrived.reshape(devices * STEPS * samp_dev, DISTINCT * block)
    fitted, residual = fit(step_rate, samp_dev, order, holder, seen, weights, targets, kept)
    return fitted[None, None], residual


def solution(mesh):
    return jax.shard_map(
        per_device,
        mesh=mesh,
        in_specs=(
            P(None, "samp", "sens"),
            P(None, "samp", None),
            P("sens", "samp", None, None, None),
            P("sens", None, None),
            P("sens", None, None),
            P("sens", None),
        ),
        out_specs=(P("sens", "samp", None, None, None), P("samp", None)),
        check_vma=False,
    )
```
